1024 devices in a mesh: gx: 16 (over z), gy: 16 (over y, core), gz: 4 (over x).
Axes of the slice: x: 4, y: 8, z: 16, core: 2. Of those that a mesh axis runs over, the one named last changes fastest.
Arguments:
- rhs_local: float32 [24576, 128], P(('gx', 'gy', 'gz')), may hold values from -46 to 46
- geom_diag: float32 [3, 24576, 128], P(None, ('gx', 'gy', 'gz')), may hold values from 0.01 to 0.05
- geom_off: float32 [3, 24576, 128], P(None, ('gx', 'gy', 'gz')), may hold values from -0.0048 to 0.0048
- mass_coef: float32 [24576, 128], P(('gx', 'gy', 'gz')), may hold values from 0.25 to 2.5
- elem_counts: int32 [1024], P(('gx', 'gy', 'gz')), may hold values from 2 to 6, as said below
Outputs:
- solution_nodes: float32 [22528, 120], P(('gx', 'gy', 'gz'))
- residual_nodes: float32 [22528, 120], P(('gx', 'gy', 'gz'))
The draws below stay inside these ranges and needn't reach their ends.
Inputs may be any that keep to these rules, and one draw needn't show every extreme that they name: `elem_counts`: every partition holds whole layers of 1 x 2 elements; partitions with the same gx index hold the same count, and their widths along gx, in elements, sum to 2 times the number of gx indices.
All inputs are finite; a program needn't handle non-finite values.
Results may differ from the reference program's by a relative error of at most 0.0003.
Values sent between devices are 32-bit elements; how exact they have to be, the bound alone decides.
A program may use at most 32 MiB of HBM per device.

```python
import math
import jax
import jax.numpy as jnp
import numpy as np
from jax import lax

ORDER = 7
EX = 2
EY = 1
EZ = 2
ITERS = 2
EXC = 3
COLS = 128
NXN = 22
NYN = 8
NZN = 15
NXG = 225
NYG = 113
NZG = 57
N_GX = 16
N_GY = 16
N_GZ = 4
DEVICES = 1024


def draw_elem_counts(key, part):
    key = jax.random.fold_in(key, 11)
    order_key, sign_key = jax.random.split(key)
    pair_count = N_GX // 2
    shuffled = jax.random.permutation(order_key, N_GX).astype(jnp.int32)
    signs = jax.random.randint(sign_key, (pair_count,), -1, 2).astype(jnp.int32)
    signs = signs.at[0].set(1)
    shifts = jnp.zeros((N_GX,), jnp.int32)
    shifts = shifts.at[shuffled[0:2 * pair_count:2]].set(signs)
    shifts = shifts.at[shuffled[1:2 * pair_count:2]].set(-signs)
    widths = EX + shifts
    return (jnp.repeat(widths, N_GY * N_GZ) * (EY * EZ)).astype(jnp.int32)


def draw_rhs_local(key, part):
    row_count = DEVICES * (EX + 1) * (ORDER + 1)
    col_count = EY * EZ * (ORDER + 1) ** 2
    values = jnp.clip(jax.random.normal(key, (row_count, col_count), jnp.float32), -6.0, 6.0)
    exponent = 0.5
    partition = jnp.arange(row_count) // ((EX + 1) * (ORDER + 1))
    along_x = (partition // (N_GY * N_GZ)).astype(jnp.float32) / max(N_GX - 1, 1)
    along_y = (partition // N_GZ % N_GY).astype(jnp.float32) / max(N_GY - 1, 1)
    along_z = (partition % N_GZ).astype(jnp.float32) / max(N_GZ - 1, 1)
    growth = jnp.exp(jnp.log(3.0) * exponent * (along_x + along_y + along_z))
    return values * growth[:, None]


def block_levels(own_key, shape, pieces, smallest, largest):
    level = 1.0
    for position, parts in pieces:
        draws = jax.random.uniform(jax.random.fold_in(jax.random.fold_in(own_key, 6), position), (parts,), jnp.float32, smallest / len(pieces), largest / len(pieces))
        level = level * jnp.repeat(jnp.exp(draws), shape[position] // parts).reshape((-1,) + (1,) * (len(shape) - 1 - position))
    return level


def setup_inputs(seed: int = 0) -> dict:
    key_list = jax.random.split(jax.random.key(seed), 6)
    rhs_local = draw_rhs_local(jax.random.fold_in(key_list[5], 71), 0)
    geom_diag = jnp.clip(jnp.exp(math.log(0.05) - 1.609438 * jax.random.uniform(key_list[1], (3, DEVICES * EXC * (ORDER + 1), COLS), jnp.float32) ** block_levels(key_list[1], (3, DEVICES * EXC * (ORDER + 1), COLS), ((1, 1024),), -0.2, 0.2)), 0.01, 0.05)
    geom_off = jnp.clip(jax.random.uniform(key_list[2], (3, DEVICES * EXC * (ORDER + 1), COLS), jnp.float32, -0.0048, 0.0048) * block_levels(key_list[2], (3, DEVICES * EXC * (ORDER + 1), COLS), ((1, 1024),), -0.4, 0.0), -0.0048, 0.0048)
    mass_coef = jnp.clip(jnp.exp(math.log(2.5) - 2.3025851 * jax.random.uniform(key_list[3], (DEVICES * EXC * (ORDER + 1), COLS), jnp.float32) ** block_levels(key_list[3], (DEVICES * EXC * (ORDER + 1), COLS), ((0, 1024),), -0.2, 0.2)), 0.25, 2.5)
    elem_counts = draw_elem_counts(jax.random.fold_in(key_list[5], 71), 0)
    return {"rhs_local": rhs_local, "geom_diag": geom_diag, "geom_off": geom_off, "mass_coef": mass_coef, "elem_counts": elem_counts}


points_gll = (-1.0, -0.8717401485096066, -0.5917001814331423, -0.2092992179024789,
              0.2092992179024789, 0.5917001814331423, 0.8717401485096066, 1.0)


def derivative_table():
    points = np.array(points_gll)
    total_points = points.shape[0]
    weights = np.ones(total_points)
    for j in range(total_points):
        for k in range(total_points):
            if k != j:
                weights[j] = weights[j] / (points[j] - points[k])
    deriv_table = np.zeros((total_points, total_points))
    for i in range(total_points):
        for j in range(total_points):
            if i != j:
                deriv_table[i, j] = weights[j] / weights[i] / (points[i] - points[j])
        deriv_table[i, i] = -np.sum(deriv_table[i])
    return deriv_table


def split_axis(grid_vals, which_axis, elements):
    head_part = lax.slice_in_dim(grid_vals, 0, ORDER * elements, axis=which_axis)
    head_part = head_part.reshape(grid_vals.shape[:which_axis] + (elements, ORDER) + grid_vals.shape[which_axis + 1:])
    tail_part = lax.slice_in_dim(grid_vals, ORDER, ORDER * elements + 1, stride=ORDER, axis=which_axis)
    return jnp.concatenate([head_part, jnp.expand_dims(tail_part, which_axis + 1)], axis=which_axis + 1)


def merge_axis(blocks, which_axis, elements):
    flat_shape = blocks.shape[:which_axis] + (ORDER * elements,) + blocks.shape[which_axis + 2:]
    head_part = lax.slice_in_dim(blocks, 0, ORDER, axis=which_axis + 1).reshape(flat_shape)
    tail_part = lax.slice_in_dim(blocks, ORDER, ORDER + 1, axis=which_axis + 1)
    zero_shape = list(tail_part.shape)
    zero_shape[which_axis + 1] = ORDER - 1
    tail_part = jnp.concatenate([jnp.zeros(tuple(zero_shape), blocks.dtype), tail_part], axis=which_axis + 1)
    tail_part = tail_part.reshape(flat_shape)
    pad_head = [(0, 0)] * len(flat_shape)
    pad_tail = [(0, 0)] * len(flat_shape)
    pad_head[which_axis] = (0, 1)
    pad_tail[which_axis] = (1, 0)
    return jnp.pad(head_part, pad_head) + jnp.pad(tail_part, pad_tail)


def to_elements(grid_vals, slot_count):
    span_y = (grid_vals.shape[1] - 1) // ORDER
    span_z = (grid_vals.shape[2] - 1) // ORDER
    return split_axis(split_axis(split_axis(grid_vals, 0, slot_count), 2, span_y), 4, span_z)


def to_grid(blocks):
    return merge_axis(merge_axis(merge_axis(blocks, 4, blocks.shape[4]), 2, blocks.shape[2]), 0, blocks.shape[0])


def element_apply(grid_vals, diag_part, off_part, mass_part, live_slots, deriv_table):
    slot_count = live_slots.shape[0]
    element_vals = to_elements(grid_vals, slot_count)
    block_shape = element_vals.shape
    highest = lax.Precision.HIGHEST
    grad_r = jnp.einsum("ai,xiyjzk->xayjzk", deriv_table, element_vals, precision=highest)
    grad_s = jnp.einsum("bj,xiyjzk->xiybzk", deriv_table, element_vals, precision=highest)
    grad_t = jnp.einsum("ck,xiyjzk->xiyjzc", deriv_table, element_vals, precision=highest)
    g_rr = diag_part[0].reshape(block_shape)
    g_ss = diag_part[1].reshape(block_shape)
    g_tt = diag_part[2].reshape(block_shape)
    g_rs = off_part[0].reshape(block_shape)
    g_rt = off_part[1].reshape(block_shape)
    g_st = off_part[2].reshape(block_shape)
    flux_r = g_rr * grad_r + g_rs * grad_s + g_rt * grad_t
    flux_s = g_rs * grad_r + g_ss * grad_s + g_st * grad_t
    flux_t = g_rt * grad_r + g_st * grad_s + g_tt * grad_t
    result = jnp.einsum("ai,xayjzk->xiyjzk", deriv_table, flux_r, precision=highest)
    result = result + jnp.einsum("bj,xiybzk->xiyjzk", deriv_table, flux_s, precision=highest)
    result = result + jnp.einsum("ck,xiyjzc->xiyjzk", deriv_table, flux_t, precision=highest)
    result = result + mass_part.reshape(block_shape) * element_vals
    result = result * live_slots.reshape(slot_count, 1, 1, 1, 1, 1)
    return to_grid(result)


def reference(rhs_local, geom_diag, geom_off, mass_coef, elem_counts):
    deriv_table = jnp.asarray(derivative_table(), jnp.float32)
    slot_count = EX + 1
    rows_part = slot_count * (ORDER + 1)
    grid_shape = (NXN, NYN, NZN)
    block_shape = (slot_count, ORDER + 1, EY, ORDER + 1, EZ, ORDER + 1)
    x_widths = (elem_counts.reshape(N_GX, N_GY * N_GZ)[:, 0] // (EY * EZ)).astype(jnp.int32)
    x_starts = (jnp.cumsum(x_widths) - x_widths).astype(jnp.int32)
    full_shape = (NXG + 2 * ORDER, NYG, NZG)
    part_ids = jnp.arange(DEVICES, dtype=jnp.int32)

    def corner(part_index):
        index_x = part_index // (N_GY * N_GZ)
        index_y = (part_index // N_GZ) % N_GY
        index_z = part_index % N_GZ
        return ((ORDER * x_starts[index_x]).astype(jnp.int32),
                (ORDER * EY * index_y).astype(jnp.int32),
                (ORDER * EZ * index_z).astype(jnp.int32))

    def live_of(part_index):
        width_here = elem_counts[part_index] // (EY * EZ)
        return (jnp.arange(slot_count) < width_here).astype(rhs_local.dtype)

    def apply_global(field_vals):
        def visit_part(summed, part_index):
            starts = corner(part_index)
            local_grid = lax.dynamic_slice(field_vals, starts, grid_shape)
            diag_part = lax.dynamic_slice_in_dim(geom_diag, part_index * rows_part, rows_part, axis=1)
            off_part = lax.dynamic_slice_in_dim(geom_off, part_index * rows_part, rows_part, axis=1)
            mass_part = lax.dynamic_slice_in_dim(mass_coef, part_index * rows_part, rows_part, axis=0)
            local_image = element_apply(local_grid, diag_part, off_part, mass_part, live_of(part_index), deriv_table)
            current = lax.dynamic_slice(summed, starts, grid_shape)
            return lax.dynamic_update_slice(summed, current + local_image, starts), None

        summed, unused = lax.scan(visit_part, jnp.zeros(full_shape, field_vals.dtype), part_ids)
        return summed

    def assemble_rhs():
        def visit_part(summed, part_index):
            starts = corner(part_index)
            rhs_part = lax.dynamic_slice_in_dim(rhs_local, part_index * rows_part, rows_part, axis=0)
            blocks = rhs_part.reshape(block_shape) * live_of(part_index).reshape(slot_count, 1, 1, 1, 1, 1)
            current = lax.dynamic_slice(summed, starts, grid_shape)
            return lax.dynamic_update_slice(summed, current + to_grid(blocks), starts), None

        summed, unused = lax.scan(visit_part, jnp.zeros(full_shape, rhs_local.dtype), part_ids)
        return summed

    def extract(field_vals):
        def cut_part(part_index):
            starts = corner(part_index)
            local_grid = lax.dynamic_slice(field_vals, starts, grid_shape)
            limit_row = ORDER * (elem_counts[part_index] // (EY * EZ))
            keep_rows = (jnp.arange(NXN) <= limit_row).astype(field_vals.dtype)
            return (local_grid * keep_rows[:, None, None]).reshape(NXN, NYN * NZN)

        return lax.map(cut_part, part_ids).reshape(DEVICES * NXN, NYN * NZN)

    rhs_field = assemble_rhs()
    solution = jnp.zeros_like(rhs_field)
    residual = rhs_field
    direction = rhs_field
    norm_now = jnp.sum(residual * residual)
    for step in range(ITERS):
        image_vals = apply_global(direction)
        step_len = norm_now / jnp.sum(direction * image_vals)
        solution = solution + step_len * direction
        residual = residual - step_len * image_vals
        if step + 1 < ITERS:
            norm_next = jnp.sum(residual * residual)
            direction = residual + (norm_next / norm_now) * direction
            norm_now = norm_next
    return extract(solution), extract(residual)
```

```python
import functools

import jax
import jax.numpy as jnp
import numpy as np
from jax import lax
from jax.experimental import pallas as pl
from jax.experimental.pallas import tpu as pltpu
from jax.sharding import PartitionSpec as P

ORDER = 7
NODES = ORDER + 1
EY = 1
EZ = 2
SLOTS = 3
ROWS = SLOTS * NODES
LANES = EY * NODES * EZ * NODES
PLANES_X = ORDER * SLOTS + 1
PLANES_YZ = (ORDER * EY + 1) * (ORDER * EZ + 1)
AXES = ("gx", "gy", "gz")
MESH = pl.DeviceIdType.MESH
F32 = jnp.float32
BF16 = jnp.bfloat16

points_gll = (
    -1.0,
    -0.8717401485096066,
    -0.5917001814331423,
    -0.2092992179024789,
    0.2092992179024789,
    0.5917001814331423,
    0.8717401485096066,
    1.0,
)

SIDES = ((-1, -1), (-1, 1), (1, -1), (1, 1), (0, -1), (0, 1), (-1, 0), (1, 0), (0, 0))


def derivative_table():
    points = np.array(points_gll)
    total_points = points.shape[0]
    weights = np.ones(total_points)
    for j in range(total_points):
        for k in range(total_points):
            if k != j:
                weights[j] = weights[j] / (points[j] - points[k])
    deriv_table = np.zeros((total_points, total_points))
    for i in range(total_points):
        for j in range(total_points):
            if i != j:
                deriv_table[i, j] = weights[j] / weights[i] / (points[i] - points[j])
        deriv_table[i, i] = -np.sum(deriv_table[i])
    return deriv_table


def tables():
    deriv = derivative_table().astype(np.float32)
    eye8, eye2 = np.eye(NODES, dtype=np.float32), np.eye(EZ, dtype=np.float32)
    along_s = np.kron(deriv, np.kron(eye2, eye8))
    along_t = np.kron(eye8, np.kron(eye2, deriv))
    forward = np.concatenate([along_s.T, along_t.T], axis=1)
    backward = np.concatenate([along_s, along_t], axis=0)

    radial = np.zeros((2 * NODES + 1, NODES, LANES), np.float32)
    for i in range(NODES):
        radial[i] = deriv[:, i][:, None]
        radial[NODES + i] = deriv[i, :][:, None]
    lanes = np.arange(LANES)
    distance = lanes // 16 + (lanes % 16 > 8)
    kept = lanes % 16 != 8
    for bit in range(4):
        for lane in lanes[kept]:
            if distance[lane] >> bit & 1:
                radial[2 * NODES, bit, lane - (distance[lane] & ((2 << bit) - 1))] = 1.0
    return forward, backward, radial


def wrapped(value, step, size):
    return lax.rem(value + (step + size), size)


def kernel(
    sizes,
    counts_ref,
    rhs_hbm,
    diag_hbm,
    off_hbm,
    mass_hbm,
    forward_hbm,
    backward_hbm,
    radial_hbm,
    solution_ref,
    residual_ref,
    rhs_ref,
    diag_ref,
    off_ref,
    mass_ref,
    forward_ref,
    backward_ref,
    forward_terms,
    backward_terms,
    radial_ref,
    outgoing,
    fields,
    edges,
    sums_out,
    sums_in,
    load_sem,
    send_sem,
    field_sem,
    edge_sem,
    sum_send_sem,
    sum_sem,
):
    here = tuple(lax.axis_index(axis) for axis in AXES)
    index_x, index_y, index_z = here

    def at(steps):
        return tuple(
            wrapped(here[i], steps[i], sizes[i]) if steps[i] else here[i] for i in range(3)
        )

    lines = []
    for axis in (0, 1, 2):
        line = []
        for step in range(1, sizes[axis]):
            steps = [0, 0, 0]
            steps[axis] = step
            line.append(tuple(steps))
        lines.append(line)

    partners = {tuple(s % n for s, n in zip(steps, sizes)) for line in lines for steps in line}
    partners |= {
        tuple(s % n for s, n in zip((dx, dy, dz), sizes))
        for dx in (-1, 0, 1)
        for dy, dz in SIDES
        if (dx, dy, dz) != (0, 0, 0)
    }
    partners = sorted(partners)
    barrier = pltpu.get_barrier_semaphore()
    for steps in partners:
        pl.semaphore_signal(barrier, inc=1, device_id=at(steps), device_id_type=MESH)

    loads = [
        pltpu.make_async_copy(source, target, load_sem.at[i])
        for i, (source, target) in enumerate(
            (
                (rhs_hbm, rhs_ref),
                (forward_hbm, forward_ref),
                (radial_hbm, radial_ref),
                (diag_hbm, diag_ref),
                (off_hbm, off_ref),
                (mass_hbm, mass_ref),
                (backward_hbm, backward_ref),
            )
        )
    ]
    for load in loads:
        load.start()

    lane = lax.broadcasted_iota(jnp.int32, (NODES, LANES), 1)
    row = lax.broadcasted_iota(jnp.int32, (NODES, LANES), 0)
    in_group = lane & 15
    zero = jnp.zeros((NODES, LANES), F32)

    keep_z = {
        1: (in_group == 0) & (index_z < sizes[2] - 1),
        -1: (in_group == 15) & (index_z > 0),
    }
    keep_y = {
        1: (lane < 16) & (index_y < sizes[1] - 1),
        -1: (lane >= LANES - 16) & (index_y > 0),
    }
    turn_z = {1: LANES - 15, -1: 15}
    turn_y = {1: 16, -1: LANES - 16}

    def tiled(function, *tiles):
        return [function(*parts) for parts in zip(*tiles)]

    def moved(tiles, turn, keep):
        return [jnp.where(keep, pltpu.roll(t, turn, 1), zero) for t in tiles]

    loads[0].wait()
    width = counts_ref[0] // (EY * EZ)
    live = [width > slot for slot in range(SLOTS)]

    def joined(tiles):
        tiles = [
            t
            + jnp.where(
                in_group == 7,
                pltpu.roll(t, LANES - 1, 1),
                jnp.where(in_group == 8, pltpu.roll(t, 1, 1), zero),
            )
            for t in tiles
        ]
        out = []
        for slot in range(SLOTS):
            total = tiles[slot]
            if slot:
                before = jnp.where(row == 0, pltpu.roll(tiles[slot - 1], 1, 0), zero)
                total = jnp.where(live[slot], total + before, zero)
            if slot + 1 < SLOTS:
                total = total + jnp.where(
                    row == NODES - 1, pltpu.roll(tiles[slot + 1], NODES - 1, 0), zero
                )
            out.append(total)
        return out

    def last_tile(tiles):
        return jnp.where(live[2], tiles[2], jnp.where(live[1], tiles[1], tiles[0]))

    def pack(turn, tiles):
        by_z = {0: tiles}
        for dz in (-1, 1):
            by_z[dz] = moved(tiles, turn_z[dz], keep_z[dz])
        for k, (dy, dz) in enumerate(SIDES):
            message = moved(by_z[dz], turn_y[dy], keep_y[dy]) if dy else by_z[dz]
            for slot in range(SLOTS):
                outgoing[turn, k, pl.ds(slot * NODES, NODES), :] = message[slot]
            outgoing[turn, k, pl.ds(ROWS, NODES), :] = last_tile(message)

    def edge_row(dx, k):
        return (16 if k == 8 else 8 * 0 + k) + ((1 if k == 8 else 8) if dx < 0 else 0)

    def send(turn):
        for k, (dy, dz) in enumerate(SIDES):
            for dx in (-1, 1):
                source = ROWS + NODES - 1 if dx > 0 else 0
                pltpu.make_async_remote_copy(
                    src_ref=outgoing.at[turn, k, pl.ds(source, 1)],
                    dst_ref=edges.at[turn, pl.ds(edge_row(dx, k), 1)],
                    send_sem=send_sem.at[turn, 1],
                    recv_sem=edge_sem.at[turn],
                    device_id=at((dx, dy, dz)),
                    device_id_type=MESH,
                ).start()
            if k < 8:
                pltpu.make_async_remote_copy(
                    src_ref=outgoing.at[turn, k, pl.ds(0, ROWS)],
                    dst_ref=fields.at[turn, pl.ds(k * ROWS, ROWS)],
                    send_sem=send_sem.at[turn, 0],
                    recv_sem=field_sem.at[turn],
                    device_id=at((0, dy, dz)),
                    device_id_type=MESH,
                ).start()

    def wait_bytes(ref, sem):
        pltpu.make_async_copy(ref, ref, sem).wait()

    def receive(turn, tiles):
        wait_bytes(edges.at[turn, pl.ds(0, 18)], edge_sem.at[turn])
        wait_bytes(fields.at[turn], field_sem.at[turn])
        before = jnp.sum(edges[turn, 0:8, :], axis=0, keepdims=True) + edges[turn, 16:17, :]
        after = jnp.sum(edges[turn, 8:16, :], axis=0, keepdims=True) + edges[turn, 17:18, :]
        before = jnp.where((row == 0) & (index_x > 0), before, zero)
        after = jnp.where((row == NODES - 1) & (index_x < sizes[0] - 1), after, zero)
        out = []
        for slot in range(SLOTS):
            parts = [
                fields[turn, pl.ds(k * ROWS + slot * NODES, NODES), :] for k in range(8)
            ]
            total = ((parts[0] + parts[1]) + (parts[2] + parts[3])) + (
                (parts[4] + parts[5]) + (parts[6] + parts[7])
            )
            if slot == 0:
                total = total + before
            is_last = live[slot] & jnp.logical_not(live[slot + 1]) if slot + 1 < SLOTS else live[slot]
            total = total + jnp.where(is_last, after, zero)
            out.append(tiles[slot] + total)
        return out

    def three_terms(values):
        high = values.astype(BF16)
        low = (values - high.astype(F32)).astype(BF16)
        return jnp.concatenate([high, low, high], axis=1)

    def rows_of(tiles):
        return jnp.concatenate(tiles, axis=0)

    def tiles_of(values):
        return [values[slot * NODES : (slot + 1) * NODES, :] for slot in range(SLOTS)]

    def along_r(tiles, first):
        out = []
        for t in tiles:
            terms = [radial_ref[first + i] * t[i : i + 1, :] for i in range(NODES)]
            out.append(
                ((terms[0] + terms[1]) + (terms[2] + terms[3]))
                + ((terms[4] + terms[5]) + (terms[6] + terms[7]))
            )
        return out

    def fluxes(tiles):
        lane_grads = jnp.dot(
            three_terms(rows_of(tiles)), forward_terms[...], preferred_element_type=F32
        )
        grad_r = along_r(tiles, 0)
        grad_s = tiles_of(lane_grads[:, :LANES])
        grad_t = tiles_of(lane_grads[:, LANES:])
        flux = ([], [], [])
        for slot in range(SLOTS):
            at_slot = pl.ds(slot * NODES, NODES)
            g_rr, g_ss, g_tt = (diag_ref[i, at_slot, :] for i in range(3))
            g_rs, g_rt, g_st = (off_ref[i, at_slot, :] for i in range(3))
            u_r, u_s, u_t = grad_r[slot], grad_s[slot], grad_t[slot]
            flux[0].append(g_rr * u_r + g_rs * u_s + g_rt * u_t)
            flux[1].append(g_rs * u_r + g_ss * u_s + g_st * u_t)
            flux[2].append(g_rt * u_r + g_st * u_s + g_tt * u_t)
        return (grad_r, grad_s, grad_t), flux

    def mass_times(tiles):
        return [mass_ref[pl.ds(slot * NODES, NODES), :] * tiles[slot] for slot in range(SLOTS)]

    def image_of(flux, mass_part):
        packed = jnp.concatenate([rows_of(flux[1]), rows_of(flux[2])], axis=1)
        lane_part = tiles_of(
            jnp.dot(three_terms(packed), backward_terms[...], preferred_element_type=F32)
        )
        return tiled(lambda a, b, c: (a + c) + b, lane_part, along_r(flux[0], NODES), mass_part)

    def dot(left, right):
        return (left[0] * right[0] + left[1] * right[1]) + left[2] * right[2]

    raw = [
        jnp.where(live[slot], rhs_ref[pl.ds(slot * NODES, NODES), :], zero)
        for slot in range(SLOTS)
    ]
    base = joined(raw)
    pack(0, base)
    for load in loads[1:]:
        load.wait()
    for matrix, terms in ((forward_ref, forward_terms), (backward_ref, backward_terms)):
        depth = matrix.shape[0]
        values = matrix[...]
        high = values.astype(BF16)
        terms[0:depth, :] = high
        terms[depth : 2 * depth, :] = high
        terms[2 * depth : 3 * depth, :] = (values - high.astype(F32)).astype(BF16)
    pl.semaphore_wait(barrier, len(partners))
    send(0)
    base = receive(0, base)

    unused, flux = fluxes(base)
    first_raw = image_of(flux, mass_times(base))
    first = joined(first_raw)
    pack(1, first)
    send(1)
    moment0 = dot(base, raw)
    moment1 = dot(base, first_raw)
    first = receive(1, first)

    moment2 = dot(first, first_raw)
    grads, flux = fluxes(first)
    mass_part = mass_times(first)
    moment3 = (dot(grads[0], flux[0]) + dot(grads[1], flux[1])) + (
        dot(grads[2], flux[2]) + dot(first, mass_part)
    )

    def halves(a, b):
        low = lane < 64
        return jnp.where(low, a, b) + pltpu.roll(jnp.where(low, b, a), 64, 1)

    odd, even = halves(moment0, moment1), halves(moment2, moment3)
    pairs = jnp.where(
        (lane & 32) != 0,
        odd + pltpu.roll(odd, 32, 1),
        even + pltpu.roll(even, LANES - 32, 1),
    )
    total = jnp.sum(pairs, axis=0, keepdims=True)

    def start_line(axis, value):
        sums_out[axis, 0:1, :] = value
        for k, steps in enumerate(lines[axis]):
            pltpu.make_async_remote_copy(
                src_ref=sums_out.at[axis, pl.ds(0, 1)],
                dst_ref=sums_in.at[axis, pl.ds(k, 1)],
                send_sem=sum_send_sem.at[axis],
                recv_sem=sum_sem.at[axis],
                device_id=at(steps),
                device_id_type=MESH,
            ).start()

    def finish_line(axis, value):
        count = len(lines[axis])
        wait_bytes(sums_in.at[axis, pl.ds(0, count)], sum_sem.at[axis])
        return value + jnp.sum(sums_in[axis, 0:count, :], axis=0, keepdims=True)

    def packed_grid(tiles):
        out = []
        for t in tiles:
            for bit in range(4):
                take = radial_ref[2 * NODES, bit : bit + 1, :] > 0.5
                t = jnp.where(take, pltpu.roll(t, LANES - (1 << bit), 1), t)
            out.append(t)
        return [
            out[0],
            jnp.where(row < NODES - 1, pltpu.roll(out[1], NODES - 1, 0), pltpu.roll(out[2], NODES - 2, 0)),
            pltpu.roll(out[2], NODES - 2, 0),
        ]

    start_line(0, total)
    second = joined(image_of(flux, mass_part))
    pack(2, second)
    send(2)
    base_grid = packed_grid(base)
    first_grid = packed_grid(first)
    total = finish_line(0, total)
    start_line(1, total)
    second_grid = packed_grid(receive(2, second))
    total = finish_line(1, total)
    start_line(2, total)
    total = finish_line(2, total)

    group = lax.broadcasted_iota(jnp.int32, (1, LANES), 1) // 32
    m2, m0, m3, m1 = (
        jnp.sum(jnp.where(group == k, total, 0.0), axis=1, keepdims=True) for k in range(4)
    )
    alpha0 = m0 / m1
    gain = (m2 / m1) * alpha0
    alpha1 = alpha0 * (gain - 1.0) / (alpha0 * (alpha0 * (m3 / m1)) - gain * gain)
    scale0 = alpha0 + alpha1 * gain
    scale1 = alpha0 * alpha1
    for slot in range(SLOTS):
        count = min(NODES, PLANES_X - slot * NODES)
        at_slot = pl.ds(slot * NODES, count)
        iterate = scale0 * base_grid[slot] - scale1 * first_grid[slot]
        rest = base_grid[slot] - scale0 * first_grid[slot] + scale1 * second_grid[slot]
        solution_ref[at_slot, :] = iterate[:count, :PLANES_YZ]
        residual_ref[at_slot, :] = rest[:count, :PLANES_YZ]

    for turn in range(3):
        wait_bytes(edges.at[turn, pl.ds(0, 18)], send_sem.at[turn, 1])
        wait_bytes(fields.at[turn], send_sem.at[turn, 0])
    for axis in range(3):
        wait_bytes(sums_in.at[axis, pl.ds(0, len(lines[axis]))], sum_send_sem.at[axis])


def local(sizes, rhs_local, geom_diag, geom_off, mass_coef, elem_counts):
    forward, backward, radial = tables()
    hbm = pl.BlockSpec(memory_space=pltpu.HBM)
    vmem = pl.BlockSpec(memory_space=pltpu.VMEM)
    out = jax.ShapeDtypeStruct((PLANES_X, PLANES_YZ), F32)
    return pl.pallas_call(
        functools.partial(kernel, sizes),
        name="cg",
        out_shape=(out, out),
        in_specs=[pl.BlockSpec(memory_space=pltpu.SMEM)] + [hbm] * 7,
        out_specs=(vmem, vmem),
        scratch_shapes=[
            pltpu.VMEM((ROWS, LANES), F32),
            pltpu.VMEM((3, ROWS, LANES), F32),
            pltpu.VMEM((3, ROWS, LANES), F32),
            pltpu.VMEM((ROWS, LANES), F32),
            pltpu.VMEM(forward.shape, F32),
            pltpu.VMEM(backward.shape, F32),
            pltpu.VMEM((3 * forward.shape[0], forward.shape[1]), BF16),
            pltpu.VMEM((3 * backward.shape[0], backward.shape[1]), BF16),
            pltpu.VMEM(radial.shape, F32),
            pltpu.VMEM((3, 9, ROWS + NODES, LANES), F32),
            pltpu.VMEM((3, 8 * ROWS, LANES), F32),
            pltpu.VMEM((3, 24, LANES), F32),
            pltpu.VMEM((3, 8, LANES), F32),
            pltpu.VMEM((3, 16, LANES), F32),
            pltpu.SemaphoreType.DMA((7,)),
            pltpu.SemaphoreType.DMA((3, 2)),
            pltpu.SemaphoreType.DMA((3,)),
            pltpu.SemaphoreType.DMA((3,)),
            pltpu.SemaphoreType.DMA((3,)),
            pltpu.SemaphoreType.DMA((3,)),
        ],
        compiler_params=pltpu.CompilerParams(
            collective_id=0, has_side_effects=True, vmem_limit_bytes=16 * 1024 * 1024
        ),
    )(
        elem_counts,
        *(
            pltpu.with_memory_space_constraint(array, pltpu.HBM)
            for array in (
                rhs_local,
                geom_diag,
                geom_off,
                mass_coef,
                jnp.asarray(forward),
                jnp.asarray(backward),
                jnp.asarray(radial),
            )
        ),
    )


def solution(mesh):
    placed = (
        P(AXES, None),
        P(None, AXES, None),
        P(None, AXES, None),
        P(AXES, None),
        P(AXES),
    )
    sizes = tuple(mesh.shape[axis] for axis in AXES)
    return jax.shard_map(
        functools.partial(local, sizes),
        mesh=mesh,
        in_specs=placed,
        out_specs=(P(AXES, None), P(AXES, None)),
        check_vma=False,
    )
```

```python
import functools

import jax
import jax.numpy as jnp
import numpy as np
from jax import lax
from jax.experimental import pallas as pl
from jax.experimental.pallas import tpu as pltpu
from jax.sharding import PartitionSpec as P

ORDER = 7
NODES = ORDER + 1
EY = 1
EZ = 2
SLOTS = 3
ROWS = SLOTS * NODES
LANES = EY * NODES * EZ * NODES
PLANES_X = ORDER * SLOTS + 1
PLANES_YZ = (ORDER * EY + 1) * (ORDER * EZ + 1)
AXES = ("gx", "gy", "gz")
MESH = pl.DeviceIdType.MESH
F32 = jnp.float32
BF16 = jnp.bfloat16

points_gll = (
    -1.0,
    -0.8717401485096066,
    -0.5917001814331423,
    -0.2092992179024789,
    0.2092992179024789,
    0.5917001814331423,
    0.8717401485096066,
    1.0,
)

SIDES = ((-1, -1), (-1, 1), (1, -1), (1, 1), (0, -1), (0, 1), (-1, 0), (1, 0), (0, 0))
NEIGHBOURS = sorted(
    ((dx, dy, dz) for dx in (-1, 0, 1) for dy, dz in SIDES if (dx, dy, dz) != (0, 0, 0)),
    key=lambda steps: -sum(map(abs, steps)),
)


def derivative_table():
    points = np.array(points_gll)
    total_points = points.shape[0]
    weights = np.ones(total_points)
    for j in range(total_points):
        for k in range(total_points):
            if k != j:
                weights[j] = weights[j] / (points[j] - points[k])
    deriv_table = np.zeros((total_points, total_points))
    for i in range(total_points):
        for j in range(total_points):
            if i != j:
                deriv_table[i, j] = weights[j] / weights[i] / (points[i] - points[j])
        deriv_table[i, i] = -np.sum(deriv_table[i])
    return deriv_table


def tables():
    deriv = derivative_table().astype(np.float32)
    eye8, eye2 = np.eye(NODES, dtype=np.float32), np.eye(EZ, dtype=np.float32)
    along_s = np.kron(deriv, np.kron(eye2, eye8))
    along_t = np.kron(eye8, np.kron(eye2, deriv))
    forward = np.concatenate([along_s.T, along_t.T], axis=1)
    backward = np.concatenate([along_s, along_t], axis=0)

    radial = np.zeros((2 * NODES + 1, NODES, LANES), np.float32)
    for i in range(NODES):
        radial[i] = deriv[:, i][:, None]
        radial[NODES + i] = deriv[i, :][:, None]
    lanes = np.arange(LANES)
    distance = lanes // 16 + (lanes % 16 > 8)
    kept = lanes % 16 != 8
    for bit in range(4):
        for lane in lanes[kept]:
            if distance[lane] >> bit & 1:
                radial[2 * NODES, bit, lane - (distance[lane] & ((2 << bit) - 1))] = 1.0
    return forward, backward, radial


def kernel(
    sizes,
    counts_ref,
    rhs_hbm,
    diag_hbm,
    off_hbm,
    mass_hbm,
    forward_hbm,
    backward_hbm,
    radial_hbm,
    fields_ref,
    rhs_ref,
    diag_ref,
    off_ref,
    mass_ref,
    forward_ref,
    backward_ref,
    forward_terms,
    backward_terms,
    radial_ref,
    outgoing,
    fields,
    edges,
    sums_out,
    sums_in,
    load_sem,
    send_sem,
    field_sem,
    edge_sem,
    sum_send_sem,
    sum_sem,
    here_sem,
):
    here = tuple(lax.axis_index(axis) for axis in AXES)
    index_x, index_y, index_z = here

    places = {}

    def at(steps):
        for axis in range(3):
            step = steps[axis] % sizes[axis]
            if (axis, step) not in places:
                moved_on = here[axis] + step
                places[axis, step] = (
                    jnp.where(moved_on >= sizes[axis], moved_on - sizes[axis], moved_on)
                    if step
                    else here[axis]
                )
        return tuple(places[axis, steps[axis] % sizes[axis]] for axis in range(3))

    def signal(semaphore, steps):
        pl.semaphore_signal(semaphore, inc=1, device_id=at(steps), device_id_type=MESH)

    lines = []
    for axis in (0, 1, 2):
        line = []
        for step in range(1, sizes[axis]):
            steps = [0, 0, 0]
            steps[axis] = step
            line.append(tuple(steps))
        lines.append(line)

    loads = [
        pltpu.make_async_copy(source, target, load_sem.at[i])
        for i, (source, target) in enumerate(
            (
                (rhs_hbm, rhs_ref),
                (forward_hbm, forward_ref),
                (radial_hbm, radial_ref),
                (diag_hbm, diag_ref),
                (off_hbm, off_ref),
                (mass_hbm, mass_ref),
                (backward_hbm, backward_ref),
            )
        )
    ]
    loads[0].start()

    barrier = pltpu.get_barrier_semaphore()
    for steps in NEIGHBOURS:
        signal(barrier, steps)

    for load in loads[1:]:
        load.start()

    lane = lax.broadcasted_iota(jnp.int32, (NODES, LANES), 1)
    row = lax.broadcasted_iota(jnp.int32, (NODES, LANES), 0)
    in_group = lane & 15
    zero = jnp.zeros((NODES, LANES), F32)

    keep_z = {
        1: (in_group == 0) & (index_z < sizes[2] - 1),
        -1: (in_group == 15) & (index_z > 0),
    }
    keep_y = {
        1: (lane < 16) & (index_y < sizes[1] - 1),
        -1: (lane >= LANES - 16) & (index_y > 0),
    }
    turn_z = {1: LANES - 15, -1: 15}
    turn_y = {1: 16, -1: LANES - 16}

    def tiled(function, *tiles):
        return [function(*parts) for parts in zip(*tiles)]

    def moved(tiles, turn, keep):
        return [jnp.where(keep, pltpu.roll(t, turn, 1), zero) for t in tiles]

    loads[0].wait()
    width = counts_ref[0] // (EY * EZ)
    live = [width > slot for slot in range(SLOTS)]

    def joined(tiles):
        tiles = [
            t
            + jnp.where(
                in_group == 7,
                pltpu.roll(t, LANES - 1, 1),
                jnp.where(in_group == 8, pltpu.roll(t, 1, 1), zero),
            )
            for t in tiles
        ]
        out = []
        for slot in range(SLOTS):
            total = tiles[slot]
            if slot:
                before = jnp.where(row == 0, pltpu.roll(tiles[slot - 1], 1, 0), zero)
                total = jnp.where(live[slot], total + before, zero)
            if slot + 1 < SLOTS:
                total = total + jnp.where(
                    row == NODES - 1, pltpu.roll(tiles[slot + 1], NODES - 1, 0), zero
                )
            out.append(total)
        return out

    def last_tile(tiles):
        return jnp.where(live[2], tiles[2], jnp.where(live[1], tiles[1], tiles[0]))

    def pack(turn, tiles):
        by_z = {0: tiles}
        for dz in (-1, 1):
            by_z[dz] = moved(tiles, turn_z[dz], keep_z[dz])
        for k, (dy, dz) in enumerate(SIDES):
            message = moved(by_z[dz], turn_y[dy], keep_y[dy]) if dy else by_z[dz]
            for slot in range(SLOTS):
                outgoing[turn, k, pl.ds(slot * NODES, NODES), :] = message[slot]
            outgoing[turn, k, pl.ds(ROWS, NODES), :] = last_tile(message)

    def edge_row(dx, k):
        row_before = 16 if k == 8 else k
        return row_before + (1 if k == 8 else 8) * (dx < 0)

    def send(turn):
        for steps in NEIGHBOURS:
            dx, k = steps[0], SIDES.index(steps[1:])
            if dx:
                source, count = (ROWS + NODES - 1 if dx > 0 else 0), 1
                target, row_to, sem, kind = edges, edge_row(dx, k), edge_sem, 1
            else:
                source, count = 0, ROWS
                target, row_to, sem, kind = fields, k * ROWS, field_sem, 0
            pltpu.make_async_remote_copy(
                src_ref=outgoing.at[turn, k, pl.ds(source, count)],
                dst_ref=target.at[turn, pl.ds(row_to, count)],
                send_sem=send_sem.at[turn, kind],
                recv_sem=sem.at[turn],
                device_id=at(steps),
                device_id_type=MESH,
            ).start()

    def wait_bytes(ref, sem):
        pltpu.make_async_copy(ref, ref, sem).wait()

    def receive(turn, tiles):
        wait_bytes(edges.at[turn, pl.ds(0, 18)], edge_sem.at[turn])
        wait_bytes(fields.at[turn], field_sem.at[turn])
        before = jnp.sum(edges[turn, 0:8, :], axis=0, keepdims=True) + edges[turn, 16:17, :]
        after = jnp.sum(edges[turn, 8:16, :], axis=0, keepdims=True) + edges[turn, 17:18, :]
        before = jnp.where((row == 0) & (index_x > 0), before, zero)
        after = jnp.where((row == NODES - 1) & (index_x < sizes[0] - 1), after, zero)
        out = []
        for slot in range(SLOTS):
            parts = [
                fields[turn, pl.ds(k * ROWS + slot * NODES, NODES), :] for k in range(8)
            ]
            total = ((parts[0] + parts[1]) + (parts[2] + parts[3])) + (
                (parts[4] + parts[5]) + (parts[6] + parts[7])
            )
            if slot == 0:
                total = total + before
            is_last = live[slot] & jnp.logical_not(live[slot + 1]) if slot + 1 < SLOTS else live[slot]
            total = total + jnp.where(is_last, after, zero)
            out.append(tiles[slot] + total)
        return out

    def three_terms(values):
        high = values.astype(BF16)
        low = (values - high.astype(F32)).astype(BF16)
        return jnp.concatenate([high, low, high], axis=1)

    def rows_of(tiles):
        return jnp.concatenate(tiles, axis=0)

    def tiles_of(values):
        return [values[slot * NODES : (slot + 1) * NODES, :] for slot in range(SLOTS)]

    def along_r(tiles, first):
        out = []
        for t in tiles:
            terms = [radial_ref[first + i] * t[i : i + 1, :] for i in range(NODES)]
            out.append(
                ((terms[0] + terms[1]) + (terms[2] + terms[3]))
                + ((terms[4] + terms[5]) + (terms[6] + terms[7]))
            )
        return out

    def fluxes(tiles):
        lane_grads = jnp.dot(
            three_terms(rows_of(tiles)), forward_terms[...], preferred_element_type=F32
        )
        grad_r = along_r(tiles, 0)
        grad_s = tiles_of(lane_grads[:, :LANES])
        grad_t = tiles_of(lane_grads[:, LANES:])
        flux = ([], [], [])
        for slot in range(SLOTS):
            at_slot = pl.ds(slot * NODES, NODES)
            g_rr, g_ss, g_tt = (diag_ref[i, at_slot, :] for i in range(3))
            g_rs, g_rt, g_st = (off_ref[i, at_slot, :] for i in range(3))
            u_r, u_s, u_t = grad_r[slot], grad_s[slot], grad_t[slot]
            flux[0].append(g_rr * u_r + g_rs * u_s + g_rt * u_t)
            flux[1].append(g_rs * u_r + g_ss * u_s + g_st * u_t)
            flux[2].append(g_rt * u_r + g_st * u_s + g_tt * u_t)
        return (grad_r, grad_s, grad_t), flux

    def mass_times(tiles):
        return [mass_ref[pl.ds(slot * NODES, NODES), :] * tiles[slot] for slot in range(SLOTS)]

    def image_of(flux, mass_part):
        packed = jnp.concatenate([rows_of(flux[1]), rows_of(flux[2])], axis=1)
        lane_part = tiles_of(
            jnp.dot(three_terms(packed), backward_terms[...], preferred_element_type=F32)
        )
        return tiled(lambda a, b, c: (a + c) + b, lane_part, along_r(flux[0], NODES), mass_part)

    def dot(left, right):
        return (left[0] * right[0] + left[1] * right[1]) + left[2] * right[2]

    raw = [
        jnp.where(live[slot], rhs_ref[pl.ds(slot * NODES, NODES), :], zero)
        for slot in range(SLOTS)
    ]
    base = joined(raw)
    pack(0, base)
    pl.semaphore_wait(barrier, len(NEIGHBOURS))
    send(0)
    for load in loads[1:]:
        load.wait()
    for matrix, terms in ((forward_ref, forward_terms), (backward_ref, backward_terms)):
        depth = matrix.shape[0]
        values = matrix[...]
        high = values.astype(BF16)
        terms[0:depth, :] = high
        terms[depth : 2 * depth, :] = high
        terms[2 * depth : 3 * depth, :] = (values - high.astype(F32)).astype(BF16)
    base = receive(0, base)

    rounds = []
    reach = 2
    while any(reach < size // 2 for size in sizes):
        rounds.append([(axis, reach) for axis in range(3) if reach < sizes[axis] // 2])
        reach *= 2

    def announce(turn):
        for axis, reach in rounds[turn]:
            for way in (0, 1):
                steps = [0, 0, 0]
                steps[axis] = reach if way else -reach
                signal(here_sem.at[turn, axis, way], steps)

    def hear(turn):
        for axis, unused_reach in rounds[turn]:
            for way in (0, 1):
                pl.semaphore_wait(here_sem.at[turn, axis, way], 1)

    if rounds:
        announce(0)

    unused, flux = fluxes(base)
    first_raw = image_of(flux, mass_times(base))
    first = joined(first_raw)
    pack(1, first)
    send(1)
    moment0 = dot(base, raw)
    moment1 = dot(base, first_raw)
    for turn in range(len(rounds)):
        hear(turn)
        if turn + 1 < len(rounds):
            announce(turn + 1)
    first = receive(1, first)

    moment2 = dot(first, first_raw)
    grads, flux = fluxes(first)
    mass_part = mass_times(first)
    moment3 = (dot(grads[0], flux[0]) + dot(grads[1], flux[1])) + (
        dot(grads[2], flux[2]) + dot(first, mass_part)
    )

    def halves(a, b):
        low = lane < 64
        return jnp.where(low, a, b) + pltpu.roll(jnp.where(low, b, a), 64, 1)

    odd, even = halves(moment0, moment1), halves(moment2, moment3)
    pairs = jnp.where(
        (lane & 32) != 0,
        odd + pltpu.roll(odd, 32, 1),
        even + pltpu.roll(even, LANES - 32, 1),
    )
    total = jnp.sum(pairs, axis=0, keepdims=True)

    def start_line(axis, value):
        sums_out[axis, 0:1, :] = value
        for k, steps in enumerate(lines[axis]):
            pltpu.make_async_remote_copy(
                src_ref=sums_out.at[axis, pl.ds(0, 1)],
                dst_ref=sums_in.at[axis, pl.ds(k, 1)],
                send_sem=sum_send_sem.at[axis],
                recv_sem=sum_sem.at[axis],
                device_id=at(steps),
                device_id_type=MESH,
            ).start()

    def finish_line(axis, value):
        count = len(lines[axis])
        wait_bytes(sums_in.at[axis, pl.ds(0, count)], sum_sem.at[axis])
        return value + jnp.sum(sums_in[axis, 0:count, :], axis=0, keepdims=True)

    def packed_grid(tiles):
        out = []
        for t in tiles:
            for bit in range(4):
                take = radial_ref[2 * NODES, bit : bit + 1, :] > 0.5
                t = jnp.where(take, pltpu.roll(t, LANES - (1 << bit), 1), t)
            out.append(t)
        return [
            out[0],
            jnp.where(row < NODES - 1, pltpu.roll(out[1], NODES - 1, 0), pltpu.roll(out[2], NODES - 2, 0)),
            pltpu.roll(out[2], NODES - 2, 0),
        ]

    def keep_grid(which, tiles):
        for slot in range(SLOTS):
            count = min(NODES, PLANES_X - slot * NODES)
            fields_ref[which, pl.ds(slot * NODES, count), :] = tiles[slot][:count, :PLANES_YZ]

    start_line(0, total)
    second = joined(image_of(flux, mass_part))
    pack(2, second)
    send(2)
    keep_grid(0, packed_grid(base))
    keep_grid(1, packed_grid(first))
    total = finish_line(0, total)
    start_line(1, total)
    keep_grid(2, packed_grid(receive(2, second)))
    total = finish_line(1, total)
    start_line(2, total)
    for turn in range(3):
        wait_bytes(edges.at[turn, pl.ds(0, 18)], send_sem.at[turn, 1])
        wait_bytes(fields.at[turn], send_sem.at[turn, 0])
    total = finish_line(2, total)

    group = lax.broadcasted_iota(jnp.int32, (1, LANES), 1) // 32
    m2, m0, m3, m1 = (
        jnp.sum(jnp.where(group == k, total, 0.0), axis=1, keepdims=True) for k in range(4)
    )
    alpha0 = m0 / m1
    gain = (m2 / m1) * alpha0
    alpha1 = alpha0 * (gain - 1.0) / (alpha0 * (alpha0 * (m3 / m1)) - gain * gain)
    scale0 = alpha0 + alpha1 * gain
    scale1 = alpha0 * alpha1
    fields_ref[3] = jnp.broadcast_to(scale0, (PLANES_X, PLANES_YZ))
    fields_ref[4] = jnp.broadcast_to(scale1, (PLANES_X, PLANES_YZ))

    for axis in range(3):
        wait_bytes(sums_in.at[axis, pl.ds(0, len(lines[axis]))], sum_send_sem.at[axis])


def local(sizes, rhs_local, geom_diag, geom_off, mass_coef, elem_counts):
    forward, backward, radial = tables()
    hbm = pl.BlockSpec(memory_space=pltpu.HBM)
    base, first, second, scale0, scale1 = pl.pallas_call(
        functools.partial(kernel, sizes),
        name="cg",
        out_shape=jax.ShapeDtypeStruct((5, PLANES_X, PLANES_YZ), F32),
        in_specs=[pl.BlockSpec(memory_space=pltpu.SMEM)] + [hbm] * 7,
        out_specs=pl.BlockSpec(memory_space=pltpu.VMEM),
        scratch_shapes=[
            pltpu.VMEM((ROWS, LANES), F32),
            pltpu.VMEM((3, ROWS, LANES), F32),
            pltpu.VMEM((3, ROWS, LANES), F32),
            pltpu.VMEM((ROWS, LANES), F32),
            pltpu.VMEM(forward.shape, F32),
            pltpu.VMEM(backward.shape, F32),
            pltpu.VMEM((3 * forward.shape[0], forward.shape[1]), BF16),
            pltpu.VMEM((3 * backward.shape[0], backward.shape[1]), BF16),
            pltpu.VMEM(radial.shape, F32),
            pltpu.VMEM((3, 9, ROWS + NODES, LANES), F32),
            pltpu.VMEM((3, 8 * ROWS, LANES), F32),
            pltpu.VMEM((3, 24, LANES), F32),
            pltpu.VMEM((3, 8, LANES), F32),
            pltpu.VMEM((3, 16, LANES), F32),
            pltpu.SemaphoreType.DMA((7,)),
            pltpu.SemaphoreType.DMA((3, 2)),
            pltpu.SemaphoreType.DMA((3,)),
            pltpu.SemaphoreType.DMA((3,)),
            pltpu.SemaphoreType.DMA((3,)),
            pltpu.SemaphoreType.DMA((3,)),
            pltpu.SemaphoreType.REGULAR((4, 3, 2)),
        ],
        compiler_params=pltpu.CompilerParams(
            collective_id=0, has_side_effects=True, vmem_limit_bytes=16 * 1024 * 1024
        ),
    )(
        elem_counts,
        *(
            pltpu.with_memory_space_constraint(array, pltpu.HBM)
            for array in (
                rhs_local,
                geom_diag,
                geom_off,
                mass_coef,
                jnp.asarray(forward),
                jnp.asarray(backward),
                jnp.asarray(radial),
            )
        ),
    )
    return scale0 * base - scale1 * first, base - scale0 * first + scale1 * second


def solution(mesh):
    placed = (
        P(AXES, None),
        P(None, AXES, None),
        P(None, AXES, None),
        P(AXES, None),
        P(AXES),
    )
    sizes = tuple(mesh.shape[axis] for axis in AXES)
    return jax.shard_map(
        functools.partial(local, sizes),
        mesh=mesh,
        in_specs=placed,
        out_specs=(P(AXES, None), P(AXES, None)),
        check_vma=False,
    )
```

```python
import functools

import jax
import jax.numpy as jnp
import numpy as np
from jax import lax
from jax.experimental import pallas as pl
from jax.experimental.pallas import tpu as pltpu
from jax.sharding import PartitionSpec as P

ORDER = 7
NODES = ORDER + 1
EY = 1
EZ = 2
SLOTS = 3
ROWS = SLOTS * NODES
LANES = EY * NODES * EZ * NODES
PLANES_X = ORDER * SLOTS + 1
PLANES_YZ = (ORDER * EY + 1) * (ORDER * EZ + 1)
AXES = ("gx", "gy", "gz")
MESH = pl.DeviceIdType.MESH
F32 = jnp.float32
BF16 = jnp.bfloat16

points_gll = (
    -1.0,
    -0.8717401485096066,
    -0.5917001814331423,
    -0.2092992179024789,
    0.2092992179024789,
    0.5917001814331423,
    0.8717401485096066,
    1.0,
)

SIDES = ((-1, -1), (-1, 1), (1, -1), (1, 1), (0, -1), (0, 1), (-1, 0), (1, 0), (0, 0))
NEIGHBOURS = sorted(
    ((dx, dy, dz) for dx in (-1, 0, 1) for dy, dz in SIDES if (dx, dy, dz) != (0, 0, 0)),
    key=lambda steps: -sum(map(abs, steps)),
)


def derivative_table():
    points = np.array(points_gll)
    total_points = points.shape[0]
    weights = np.ones(total_points)
    for j in range(total_points):
        for k in range(total_points):
            if k != j:
                weights[j] = weights[j] / (points[j] - points[k])
    deriv_table = np.zeros((total_points, total_points))
    for i in range(total_points):
        for j in range(total_points):
            if i != j:
                deriv_table[i, j] = weights[j] / weights[i] / (points[i] - points[j])
        deriv_table[i, i] = -np.sum(deriv_table[i])
    return deriv_table


def tables():
    deriv = derivative_table().astype(np.float32)
    eye8, eye2 = np.eye(NODES, dtype=np.float32), np.eye(EZ, dtype=np.float32)
    along_s = np.kron(deriv, np.kron(eye2, eye8))
    along_t = np.kron(eye8, np.kron(eye2, deriv))
    forward = np.concatenate([along_s.T, along_t.T], axis=1)
    backward = np.concatenate([along_s, along_t], axis=0)

    radial = np.zeros((2 * NODES + 1, NODES, LANES), np.float32)
    for i in range(NODES):
        radial[i] = deriv[:, i][:, None]
        radial[NODES + i] = deriv[i, :][:, None]
    lanes = np.arange(LANES)
    distance = lanes // 16 + (lanes % 16 > 8)
    kept = lanes % 16 != 8
    for bit in range(4):
        for lane in lanes[kept]:
            if distance[lane] >> bit & 1:
                radial[2 * NODES, bit, lane - (distance[lane] & ((2 << bit) - 1))] = 1.0
    return forward, backward, radial


def kernel(
    sizes,
    counts_ref,
    rhs_hbm,
    diag_hbm,
    off_hbm,
    mass_hbm,
    forward_hbm,
    backward_hbm,
    radial_hbm,
    fields_ref,
    rhs_ref,
    diag_ref,
    off_ref,
    mass_ref,
    forward_ref,
    backward_ref,
    forward_terms,
    backward_terms,
    radial_ref,
    outgoing,
    fields,
    edges,
    sums_out,
    sums_in,
    load_sem,
    send_sem,
    field_sem,
    edge_sem,
    sum_send_sem,
    sum_sem,
    here_sem,
):
    here = tuple(lax.axis_index(axis) for axis in AXES)
    index_x, index_y, index_z = here

    places = {}

    def at(steps):
        for axis in range(3):
            step = steps[axis] % sizes[axis]
            if (axis, step) not in places:
                moved_on = here[axis] + step
                places[axis, step] = (
                    jnp.where(moved_on >= sizes[axis], moved_on - sizes[axis], moved_on)
                    if step
                    else here[axis]
                )
        return tuple(places[axis, steps[axis] % sizes[axis]] for axis in range(3))

    def signal(semaphore, steps):
        pl.semaphore_signal(semaphore, inc=1, device_id=at(steps), device_id_type=MESH)

    def distance(steps):
        around = [min(step % size, -step % size) for step, size in zip(steps, sizes)]
        return around[0] + around[1] / 2 + around[2]

    groups = [
        sorted(((step, 0, 0) for step in range(1, sizes[0])), key=distance, reverse=True),
        sorted(
            (
                (0, step_y, step_z)
                for step_y in range(sizes[1])
                for step_z in range(sizes[2])
                if step_y or step_z
            ),
            key=distance,
            reverse=True,
        ),
    ]

    loads = [
        pltpu.make_async_copy(source, target, load_sem.at[i])
        for i, (source, target) in enumerate(
            (
                (rhs_hbm, rhs_ref),
                (forward_hbm, forward_ref),
                (radial_hbm, radial_ref),
                (diag_hbm, diag_ref),
                (off_hbm, off_ref),
                (mass_hbm, mass_ref),
                (backward_hbm, backward_ref),
            )
        )
    ]
    loads[0].start()

    barrier = pltpu.get_barrier_semaphore()
    for steps in NEIGHBOURS:
        signal(barrier, steps)

    for load in loads[1:]:
        load.start()

    lane = lax.broadcasted_iota(jnp.int32, (NODES, LANES), 1)
    row = lax.broadcasted_iota(jnp.int32, (NODES, LANES), 0)
    in_group = lane & 15
    zero = jnp.zeros((NODES, LANES), F32)

    keep_z = {
        1: (in_group == 0) & (index_z < sizes[2] - 1),
        -1: (in_group == 15) & (index_z > 0),
    }
    keep_y = {
        1: (lane < 16) & (index_y < sizes[1] - 1),
        -1: (lane >= LANES - 16) & (index_y > 0),
    }
    turn_z = {1: LANES - 15, -1: 15}
    turn_y = {1: 16, -1: LANES - 16}

    def tiled(function, *tiles):
        return [function(*parts) for parts in zip(*tiles)]

    def moved(tiles, turn, keep):
        return [jnp.where(keep, pltpu.roll(t, turn, 1), zero) for t in tiles]

    loads[0].wait()
    width = counts_ref[0] // (EY * EZ)
    live = [width > slot for slot in range(SLOTS)]

    def joined(tiles):
        tiles = [
            t
            + jnp.where(
                in_group == 7,
                pltpu.roll(t, LANES - 1, 1),
                jnp.where(in_group == 8, pltpu.roll(t, 1, 1), zero),
            )
            for t in tiles
        ]
        out = []
        for slot in range(SLOTS):
            total = tiles[slot]
            if slot:
                before = jnp.where(row == 0, pltpu.roll(tiles[slot - 1], 1, 0), zero)
                total = jnp.where(live[slot], total + before, zero)
            if slot + 1 < SLOTS:
                total = total + jnp.where(
                    row == NODES - 1, pltpu.roll(tiles[slot + 1], NODES - 1, 0), zero
                )
            out.append(total)
        return out

    def last_tile(tiles):
        return jnp.where(live[2], tiles[2], jnp.where(live[1], tiles[1], tiles[0]))

    def pack(turn, tiles):
        by_z = {0: tiles}
        for dz in (-1, 1):
            by_z[dz] = moved(tiles, turn_z[dz], keep_z[dz])
        for k, (dy, dz) in enumerate(SIDES):
            message = moved(by_z[dz], turn_y[dy], keep_y[dy]) if dy else by_z[dz]
            for slot in range(SLOTS):
                outgoing[turn, k, pl.ds(slot * NODES, NODES), :] = message[slot]
            outgoing[turn, k, pl.ds(ROWS, NODES), :] = last_tile(message)

    def edge_row(dx, k):
        row_before = 16 if k == 8 else k
        return row_before + (1 if k == 8 else 8) * (dx < 0)

    def send(turn):
        for steps in NEIGHBOURS:
            dx, k = steps[0], SIDES.index(steps[1:])
            if dx:
                source, count = (ROWS + NODES - 1 if dx > 0 else 0), 1
                target, row_to, sem, kind = edges, edge_row(dx, k), edge_sem, 1
            else:
                source, count = 0, ROWS
                target, row_to, sem, kind = fields, k * ROWS, field_sem, 0
            pltpu.make_async_remote_copy(
                src_ref=outgoing.at[turn, k, pl.ds(source, count)],
                dst_ref=target.at[turn, pl.ds(row_to, count)],
                send_sem=send_sem.at[turn, kind],
                recv_sem=sem.at[turn],
                device_id=at(steps),
                device_id_type=MESH,
            ).start()

    def wait_bytes(ref, sem):
        pltpu.make_async_copy(ref, ref, sem).wait()

    def receive(turn, tiles):
        wait_bytes(edges.at[turn, pl.ds(0, 18)], edge_sem.at[turn])
        wait_bytes(fields.at[turn], field_sem.at[turn])
        before = jnp.sum(edges[turn, 0:8, :], axis=0, keepdims=True) + edges[turn, 16:17, :]
        after = jnp.sum(edges[turn, 8:16, :], axis=0, keepdims=True) + edges[turn, 17:18, :]
        before = jnp.where((row == 0) & (index_x > 0), before, zero)
        after = jnp.where((row == NODES - 1) & (index_x < sizes[0] - 1), after, zero)
        out = []
        for slot in range(SLOTS):
            parts = [
                fields[turn, pl.ds(k * ROWS + slot * NODES, NODES), :] for k in range(8)
            ]
            total = ((parts[0] + parts[1]) + (parts[2] + parts[3])) + (
                (parts[4] + parts[5]) + (parts[6] + parts[7])
            )
            if slot == 0:
                total = total + before
            is_last = live[slot] & jnp.logical_not(live[slot + 1]) if slot + 1 < SLOTS else live[slot]
            total = total + jnp.where(is_last, after, zero)
            out.append(tiles[slot] + total)
        return out

    def three_terms(values):
        high = values.astype(BF16)
        low = (values - high.astype(F32)).astype(BF16)
        return jnp.concatenate([high, low, high], axis=1)

    def rows_of(tiles):
        return jnp.concatenate(tiles, axis=0)

    def tiles_of(values):
        return [values[slot * NODES : (slot + 1) * NODES, :] for slot in range(SLOTS)]

    def along_r(tiles, first):
        out = []
        for t in tiles:
            terms = [radial_ref[first + i] * t[i : i + 1, :] for i in range(NODES)]
            out.append(
                ((terms[0] + terms[1]) + (terms[2] + terms[3]))
                + ((terms[4] + terms[5]) + (terms[6] + terms[7]))
            )
        return out

    def fluxes(tiles):
        lane_grads = jnp.dot(
            three_terms(rows_of(tiles)), forward_terms[...], preferred_element_type=F32
        )
        grad_r = along_r(tiles, 0)
        grad_s = tiles_of(lane_grads[:, :LANES])
        grad_t = tiles_of(lane_grads[:, LANES:])
        flux = ([], [], [])
        for slot in range(SLOTS):
            at_slot = pl.ds(slot * NODES, NODES)
            g_rr, g_ss, g_tt = (diag_ref[i, at_slot, :] for i in range(3))
            g_rs, g_rt, g_st = (off_ref[i, at_slot, :] for i in range(3))
            u_r, u_s, u_t = grad_r[slot], grad_s[slot], grad_t[slot]
            flux[0].append(g_rr * u_r + g_rs * u_s + g_rt * u_t)
            flux[1].append(g_rs * u_r + g_ss * u_s + g_st * u_t)
            flux[2].append(g_rt * u_r + g_st * u_s + g_tt * u_t)
        return (grad_r, grad_s, grad_t), flux

    def mass_times(tiles):
        return [mass_ref[pl.ds(slot * NODES, NODES), :] * tiles[slot] for slot in range(SLOTS)]

    def image_of(flux, mass_part):
        packed = jnp.concatenate([rows_of(flux[1]), rows_of(flux[2])], axis=1)
        lane_part = tiles_of(
            jnp.dot(three_terms(packed), backward_terms[...], preferred_element_type=F32)
        )
        return tiled(lambda a, b, c: (a + c) + b, lane_part, along_r(flux[0], NODES), mass_part)

    def dot(left, right):
        return (left[0] * right[0] + left[1] * right[1]) + left[2] * right[2]

    raw = [
        jnp.where(live[slot], rhs_ref[pl.ds(slot * NODES, NODES), :], zero)
        for slot in range(SLOTS)
    ]
    base = joined(raw)
    pack(0, base)
    pl.semaphore_wait(barrier, len(NEIGHBOURS))
    send(0)
    for load in loads[1:]:
        load.wait()
    for matrix, terms in ((forward_ref, forward_terms), (backward_ref, backward_terms)):
        depth = matrix.shape[0]
        values = matrix[...]
        high = values.astype(BF16)
        terms[0:depth, :] = high
        terms[depth : 2 * depth, :] = high
        terms[2 * depth : 3 * depth, :] = (values - high.astype(F32)).astype(BF16)
    base = receive(0, base)

    rounds = []
    reach = 2
    while any(reach < size // 2 for size in sizes):
        rounds.append([(axis, reach) for axis in range(3) if reach < sizes[axis] // 2])
        reach *= 2

    def announce(turn):
        for axis, reach in rounds[turn]:
            for way in (0, 1):
                steps = [0, 0, 0]
                steps[axis] = reach if way else -reach
                signal(here_sem.at[turn, axis, way], steps)

    def hear(turn):
        for axis, unused_reach in rounds[turn]:
            for way in (0, 1):
                pl.semaphore_wait(here_sem.at[turn, axis, way], 1)

    if rounds:
        announce(0)

    unused, flux = fluxes(base)
    first_raw = image_of(flux, mass_times(base))
    first = joined(first_raw)
    pack(1, first)
    send(1)
    moment0 = dot(base, raw)
    moment1 = dot(base, first_raw)
    for turn in range(len(rounds)):
        hear(turn)
        if turn + 1 < len(rounds):
            announce(turn + 1)
    first = receive(1, first)

    moment2 = dot(first, first_raw)
    grads, flux = fluxes(first)
    mass_part = mass_times(first)
    moment3 = (dot(grads[0], flux[0]) + dot(grads[1], flux[1])) + (
        dot(grads[2], flux[2]) + dot(first, mass_part)
    )

    def halves(a, b):
        low = lane < 64
        return jnp.where(low, a, b) + pltpu.roll(jnp.where(low, b, a), 64, 1)

    odd, even = halves(moment0, moment1), halves(moment2, moment3)
    pairs = jnp.where(
        (lane & 32) != 0,
        odd + pltpu.roll(odd, 32, 1),
        even + pltpu.roll(even, LANES - 32, 1),
    )
    total = jnp.sum(pairs, axis=0, keepdims=True)

    def start_group(axis, value):
        sums_out[axis, 0:1, :] = value
        for k, steps in enumerate(groups[axis]):
            pltpu.make_async_remote_copy(
                src_ref=sums_out.at[axis, pl.ds(0, 1)],
                dst_ref=sums_in.at[axis, pl.ds(k, 1)],
                send_sem=sum_send_sem.at[axis],
                recv_sem=sum_sem.at[axis],
                device_id=at(steps),
                device_id_type=MESH,
            ).start()

    def finish_group(axis, value):
        count = len(groups[axis])
        wait_bytes(sums_in.at[axis, pl.ds(0, count)], sum_sem.at[axis])
        return value + jnp.sum(sums_in[axis, 0:count, :], axis=0, keepdims=True)

    def packed_grid(tiles):
        out = []
        for t in tiles:
            for bit in range(4):
                take = radial_ref[2 * NODES, bit : bit + 1, :] > 0.5
                t = jnp.where(take, pltpu.roll(t, LANES - (1 << bit), 1), t)
            out.append(t)
        return [
            out[0],
            jnp.where(row < NODES - 1, pltpu.roll(out[1], NODES - 1, 0), pltpu.roll(out[2], NODES - 2, 0)),
            pltpu.roll(out[2], NODES - 2, 0),
        ]

    def keep_grid(which, tiles):
        for slot in range(SLOTS):
            count = min(NODES, PLANES_X - slot * NODES)
            fields_ref[which, pl.ds(slot * NODES, count), :] = tiles[slot][:count, :PLANES_YZ]

    start_group(0, total)
    second = joined(image_of(flux, mass_part))
    pack(2, second)
    send(2)
    keep_grid(0, packed_grid(base))
    keep_grid(1, packed_grid(first))
    total = finish_group(0, total)
    start_group(1, total)
    keep_grid(2, packed_grid(receive(2, second)))
    for turn in range(3):
        wait_bytes(edges.at[turn, pl.ds(0, 18)], send_sem.at[turn, 1])
        wait_bytes(fields.at[turn], send_sem.at[turn, 0])
    total = finish_group(1, total)

    group = lax.broadcasted_iota(jnp.int32, (1, LANES), 1) // 32
    m2, m0, m3, m1 = (
        jnp.sum(jnp.where(group == k, total, 0.0), axis=1, keepdims=True) for k in range(4)
    )
    alpha0 = m0 / m1
    gain = (m2 / m1) * alpha0
    alpha1 = alpha0 * (gain - 1.0) / (alpha0 * (alpha0 * (m3 / m1)) - gain * gain)
    scale0 = alpha0 + alpha1 * gain
    scale1 = alpha0 * alpha1
    fields_ref[3] = jnp.broadcast_to(scale0, (PLANES_X, PLANES_YZ))
    fields_ref[4] = jnp.broadcast_to(scale1, (PLANES_X, PLANES_YZ))

    for axis in range(2):
        wait_bytes(sums_in.at[axis, pl.ds(0, len(groups[axis]))], sum_send_sem.at[axis])


def local(sizes, rhs_local, geom_diag, geom_off, mass_coef, elem_counts):
    forward, backward, radial = tables()
    hbm = pl.BlockSpec(memory_space=pltpu.HBM)
    base, first, second, scale0, scale1 = pl.pallas_call(
        functools.partial(kernel, sizes),
        name="cg",
        out_shape=jax.ShapeDtypeStruct((5, PLANES_X, PLANES_YZ), F32),
        in_specs=[pl.BlockSpec(memory_space=pltpu.SMEM)] + [hbm] * 7,
        out_specs=pl.BlockSpec(memory_space=pltpu.VMEM),
        scratch_shapes=[
            pltpu.VMEM((ROWS, LANES), F32),
            pltpu.VMEM((3, ROWS, LANES), F32),
            pltpu.VMEM((3, ROWS, LANES), F32),
            pltpu.VMEM((ROWS, LANES), F32),
            pltpu.VMEM(forward.shape, F32),
            pltpu.VMEM(backward.shape, F32),
            pltpu.VMEM((3 * forward.shape[0], forward.shape[1]), BF16),
            pltpu.VMEM((3 * backward.shape[0], backward.shape[1]), BF16),
            pltpu.VMEM(radial.shape, F32),
            pltpu.VMEM((3, 9, ROWS + NODES, LANES), F32),
            pltpu.VMEM((3, 8 * ROWS, LANES), F32),
            pltpu.VMEM((3, 24, LANES), F32),
            pltpu.VMEM((2, 8, LANES), F32),
            pltpu.VMEM((2, 64, LANES), F32),
            pltpu.SemaphoreType.DMA((7,)),
            pltpu.SemaphoreType.DMA((3, 2)),
            pltpu.SemaphoreType.DMA((3,)),
            pltpu.SemaphoreType.DMA((3,)),
            pltpu.SemaphoreType.DMA((3,)),
            pltpu.SemaphoreType.DMA((3,)),
            pltpu.SemaphoreType.REGULAR((4, 3, 2)),
        ],
        compiler_params=pltpu.CompilerParams(
            collective_id=0, has_side_effects=True, vmem_limit_bytes=16 * 1024 * 1024
        ),
    )(
        elem_counts,
        *(
            pltpu.with_memory_space_constraint(array, pltpu.HBM)
            for array in (
                rhs_local,
                geom_diag,
                geom_off,
                mass_coef,
                jnp.asarray(forward),
                jnp.asarray(backward),
                jnp.asarray(radial),
            )
        ),
    )
    return scale0 * base - scale1 * first, base - scale0 * first + scale1 * second


def solution(mesh):
    placed = (
        P(AXES, None),
        P(None, AXES, None),
        P(None, AXES, None),
        P(AXES, None),
        P(AXES),
    )
    sizes = tuple(mesh.shape[axis] for axis in AXES)
    return jax.shard_map(
        functools.partial(local, sizes),
        mesh=mesh,
        in_specs=placed,
        out_specs=(P(AXES, None), P(AXES, None)),
        check_vma=False,
    )
```

```python
import functools

import jax
import jax.numpy as jnp
import numpy as np
from jax import lax
from jax.experimental import pallas as pl
from jax.experimental.pallas import tpu as pltpu
from jax.sharding import PartitionSpec as P

ORDER = 7
NODES = ORDER + 1
EY = 1
EZ = 2
SLOTS = 3
ROWS = SLOTS * NODES
LANES = EY * NODES * EZ * NODES
PLANES_X = ORDER * SLOTS + 1
PLANES_YZ = (ORDER * EY + 1) * (ORDER * EZ + 1)
AXES = ("gx", "gy", "gz")
MESH = pl.DeviceIdType.MESH
F32 = jnp.float32
BF16 = jnp.bfloat16

points_gll = (
    -1.0,
    -0.8717401485096066,
    -0.5917001814331423,
    -0.2092992179024789,
    0.2092992179024789,
    0.5917001814331423,
    0.8717401485096066,
    1.0,
)

SIDES = ((-1, -1), (-1, 1), (1, -1), (1, 1), (0, -1), (0, 1), (-1, 0), (1, 0), (0, 0))
NEIGHBOURS = sorted(
    ((dx, dy, dz) for dx in (-1, 0, 1) for dy, dz in SIDES if (dx, dy, dz) != (0, 0, 0)),
    key=lambda steps: -sum(map(abs, steps)),
)


def derivative_table():
    points = np.array(points_gll)
    total_points = points.shape[0]
    weights = np.ones(total_points)
    for j in range(total_points):
        for k in range(total_points):
            if k != j:
                weights[j] = weights[j] / (points[j] - points[k])
    deriv_table = np.zeros((total_points, total_points))
    for i in range(total_points):
        for j in range(total_points):
            if i != j:
                deriv_table[i, j] = weights[j] / weights[i] / (points[i] - points[j])
        deriv_table[i, i] = -np.sum(deriv_table[i])
    return deriv_table


def tables():
    deriv = derivative_table().astype(np.float32)
    eye8, eye2 = np.eye(NODES, dtype=np.float32), np.eye(EZ, dtype=np.float32)
    along_s = np.kron(deriv, np.kron(eye2, eye8))
    along_t = np.kron(eye8, np.kron(eye2, deriv))
    forward = np.concatenate([along_s.T, along_t.T], axis=1)
    backward = np.concatenate([along_s, along_t], axis=0)

    radial = np.zeros((2 * NODES + 1, NODES, LANES), np.float32)
    for i in range(NODES):
        radial[i] = deriv[:, i][:, None]
        radial[NODES + i] = deriv[i, :][:, None]
    lanes = np.arange(LANES)
    distance = lanes // 16 + (lanes % 16 > 8)
    kept = lanes % 16 != 8
    for bit in range(4):
        for lane in lanes[kept]:
            if distance[lane] >> bit & 1:
                radial[2 * NODES, bit, lane - (distance[lane] & ((2 << bit) - 1))] = 1.0
    return forward, backward, radial


def kernel(
    sizes,
    counts_ref,
    rhs_hbm,
    diag_hbm,
    off_hbm,
    mass_hbm,
    forward_hbm,
    backward_hbm,
    radial_hbm,
    fields_ref,
    rhs_ref,
    diag_ref,
    off_ref,
    mass_ref,
    forward_ref,
    backward_ref,
    forward_terms,
    backward_terms,
    radial_ref,
    outgoing,
    fields,
    edges,
    sums_out,
    sums_in,
    load_sem,
    send_sem,
    field_sem,
    edge_sem,
    sum_send_sem,
    sum_sem,
    here_sem,
):
    here = tuple(lax.axis_index(axis) for axis in AXES)
    index_x, index_y, index_z = here

    places = {}

    def at(steps):
        for axis in range(3):
            step = steps[axis] % sizes[axis]
            if (axis, step) not in places:
                moved_on = here[axis] + step
                places[axis, step] = (
                    jnp.where(moved_on >= sizes[axis], moved_on - sizes[axis], moved_on)
                    if step
                    else here[axis]
                )
        place = [places[axis, steps[axis] % sizes[axis]] for axis in range(3)]
        if len(steps) == 4:
            place[1] = index_y + 1 - 2 * lax.rem(index_y, 2)
        return tuple(place)

    def signal(semaphore, steps):
        pl.semaphore_signal(semaphore, inc=1, device_id=at(steps), device_id_type=MESH)

    def distance(steps):
        around = [min(step % size, -step % size) for step, size in zip(steps, sizes)]
        return around[0] + around[1] / 2 + around[2]

    groups = [
        sorted(
            [(step, 0, 0) for step in range(1, sizes[0])]
            + [(step, 0, 0, 1) for step in range(sizes[0])],
            key=distance,
            reverse=True,
        ),
        sorted(
            (
                (0, step_y, step_z)
                for step_y in range(0, sizes[1], 2)
                for step_z in range(sizes[2])
                if step_y or step_z
            ),
            key=distance,
            reverse=True,
        ),
    ]

    loads = [
        pltpu.make_async_copy(source, target, load_sem.at[i])
        for i, (source, target) in enumerate(
            (
                (rhs_hbm, rhs_ref),
                (forward_hbm, forward_ref),
                (radial_hbm, radial_ref),
                (diag_hbm, diag_ref),
                (off_hbm, off_ref),
                (mass_hbm, mass_ref),
                (backward_hbm, backward_ref),
            )
        )
    ]
    loads[0].start()

    taken = {tuple(step % size for step, size in zip(steps, sizes)) for steps in NEIGHBOURS}
    greeted = NEIGHBOURS + [
        (0, step_y, step_z)
        for step_y in (-1, 0, 1)
        for step_z in range(2, sizes[2] - 1)
        if (0, step_y % sizes[1], step_z) not in taken
    ]
    barrier = pltpu.get_barrier_semaphore()
    for steps in greeted:
        signal(barrier, steps)

    for load in loads[1:]:
        load.start()

    lane = lax.broadcasted_iota(jnp.int32, (NODES, LANES), 1)
    row = lax.broadcasted_iota(jnp.int32, (NODES, LANES), 0)
    in_group = lane & 15
    zero = jnp.zeros((NODES, LANES), F32)

    keep_z = {
        1: (in_group == 0) & (index_z < sizes[2] - 1),
        -1: (in_group == 15) & (index_z > 0),
    }
    keep_y = {
        1: (lane < 16) & (index_y < sizes[1] - 1),
        -1: (lane >= LANES - 16) & (index_y > 0),
    }
    turn_z = {1: LANES - 15, -1: 15}
    turn_y = {1: 16, -1: LANES - 16}

    def tiled(function, *tiles):
        return [function(*parts) for parts in zip(*tiles)]

    def moved(tiles, turn, keep):
        return [jnp.where(keep, pltpu.roll(t, turn, 1), zero) for t in tiles]

    loads[0].wait()
    width = counts_ref[0] // (EY * EZ)
    live = [width > slot for slot in range(SLOTS)]

    def joined(tiles):
        tiles = [
            t
            + jnp.where(
                in_group == 7,
                pltpu.roll(t, LANES - 1, 1),
                jnp.where(in_group == 8, pltpu.roll(t, 1, 1), zero),
            )
            for t in tiles
        ]
        out = []
        for slot in range(SLOTS):
            total = tiles[slot]
            if slot:
                before = jnp.where(row == 0, pltpu.roll(tiles[slot - 1], 1, 0), zero)
                total = jnp.where(live[slot], total + before, zero)
            if slot + 1 < SLOTS:
                total = total + jnp.where(
                    row == NODES - 1, pltpu.roll(tiles[slot + 1], NODES - 1, 0), zero
                )
            out.append(total)
        return out

    def last_tile(tiles):
        return jnp.where(live[2], tiles[2], jnp.where(live[1], tiles[1], tiles[0]))

    def pack(turn, tiles):
        by_z = {0: tiles}
        for dz in (-1, 1):
            by_z[dz] = moved(tiles, turn_z[dz], keep_z[dz])
        for k, (dy, dz) in enumerate(SIDES):
            message = moved(by_z[dz], turn_y[dy], keep_y[dy]) if dy else by_z[dz]
            for slot in range(SLOTS):
                outgoing[turn, k, pl.ds(slot * NODES, NODES), :] = message[slot]
            outgoing[turn, k, pl.ds(ROWS, NODES), :] = last_tile(message)

    def edge_row(dx, k):
        row_before = 16 if k == 8 else k
        return row_before + (1 if k == 8 else 8) * (dx < 0)

    def send(turn):
        for steps in NEIGHBOURS:
            dx, k = steps[0], SIDES.index(steps[1:])
            if dx:
                source, count = (ROWS + NODES - 1 if dx > 0 else 0), 1
                target, row_to, sem, kind = edges, edge_row(dx, k), edge_sem, 1
            else:
                source, count = 0, ROWS
                target, row_to, sem, kind = fields, k * ROWS, field_sem, 0
            pltpu.make_async_remote_copy(
                src_ref=outgoing.at[turn, k, pl.ds(source, count)],
                dst_ref=target.at[turn, pl.ds(row_to, count)],
                send_sem=send_sem.at[turn, kind],
                recv_sem=sem.at[turn],
                device_id=at(steps),
                device_id_type=MESH,
            ).start()

    def wait_bytes(ref, sem):
        pltpu.make_async_copy(ref, ref, sem).wait()

    def receive(turn, tiles):
        wait_bytes(edges.at[turn, pl.ds(0, 18)], edge_sem.at[turn])
        wait_bytes(fields.at[turn], field_sem.at[turn])
        before = jnp.sum(edges[turn, 0:8, :], axis=0, keepdims=True) + edges[turn, 16:17, :]
        after = jnp.sum(edges[turn, 8:16, :], axis=0, keepdims=True) + edges[turn, 17:18, :]
        before = jnp.where((row == 0) & (index_x > 0), before, zero)
        after = jnp.where((row == NODES - 1) & (index_x < sizes[0] - 1), after, zero)
        out = []
        for slot in range(SLOTS):
            parts = [
                fields[turn, pl.ds(k * ROWS + slot * NODES, NODES), :] for k in range(8)
            ]
            total = ((parts[0] + parts[1]) + (parts[2] + parts[3])) + (
                (parts[4] + parts[5]) + (parts[6] + parts[7])
            )
            if slot == 0:
                total = total + before
            is_last = live[slot] & jnp.logical_not(live[slot + 1]) if slot + 1 < SLOTS else live[slot]
            total = total + jnp.where(is_last, after, zero)
            out.append(tiles[slot] + total)
        return out

    def three_terms(values):
        high = values.astype(BF16)
        low = (values - high.astype(F32)).astype(BF16)
        return jnp.concatenate([high, low, high], axis=1)

    def rows_of(tiles):
        return jnp.concatenate(tiles, axis=0)

    def tiles_of(values):
        return [values[slot * NODES : (slot + 1) * NODES, :] for slot in range(SLOTS)]

    def along_r(tiles, first):
        out = []
        for t in tiles:
            terms = [radial_ref[first + i] * t[i : i + 1, :] for i in range(NODES)]
            out.append(
                ((terms[0] + terms[1]) + (terms[2] + terms[3]))
                + ((terms[4] + terms[5]) + (terms[6] + terms[7]))
            )
        return out

    def fluxes(tiles):
        lane_grads = jnp.dot(
            three_terms(rows_of(tiles)), forward_terms[...], preferred_element_type=F32
        )
        grad_r = along_r(tiles, 0)
        grad_s = tiles_of(lane_grads[:, :LANES])
        grad_t = tiles_of(lane_grads[:, LANES:])
        flux = ([], [], [])
        for slot in range(SLOTS):
            at_slot = pl.ds(slot * NODES, NODES)
            g_rr, g_ss, g_tt = (diag_ref[i, at_slot, :] for i in range(3))
            g_rs, g_rt, g_st = (off_ref[i, at_slot, :] for i in range(3))
            u_r, u_s, u_t = grad_r[slot], grad_s[slot], grad_t[slot]
            flux[0].append(g_rr * u_r + g_rs * u_s + g_rt * u_t)
            flux[1].append(g_rs * u_r + g_ss * u_s + g_st * u_t)
            flux[2].append(g_rt * u_r + g_st * u_s + g_tt * u_t)
        return (grad_r, grad_s, grad_t), flux

    def mass_times(tiles):
        return [mass_ref[pl.ds(slot * NODES, NODES), :] * tiles[slot] for slot in range(SLOTS)]

    def image_of(flux, mass_part):
        packed = jnp.concatenate([rows_of(flux[1]), rows_of(flux[2])], axis=1)
        lane_part = tiles_of(
            jnp.dot(three_terms(packed), backward_terms[...], preferred_element_type=F32)
        )
        return tiled(lambda a, b, c: (a + c) + b, lane_part, along_r(flux[0], NODES), mass_part)

    def dot(left, right):
        return (left[0] * right[0] + left[1] * right[1]) + left[2] * right[2]

    raw = [
        jnp.where(live[slot], rhs_ref[pl.ds(slot * NODES, NODES), :], zero)
        for slot in range(SLOTS)
    ]
    base = joined(raw)
    pack(0, base)
    pl.semaphore_wait(barrier, len(greeted))
    send(0)
    rounds = []
    reach = 1
    while any(reach < size // 2 for size in sizes[:2]):
        rounds.append([(axis, reach) for axis in (0, 1) if reach < sizes[axis] // 2])
        reach *= 2

    def announce(turn):
        for axis, reach in rounds[turn]:
            for way in (0, 1):
                steps = [0, 0, 0]
                steps[axis] = reach if way else -reach
                signal(here_sem.at[turn, axis, way], steps)

    def hear(turn):
        for axis, unused_reach in rounds[turn]:
            for way in (0, 1):
                pl.semaphore_wait(here_sem.at[turn, axis, way], 1)

    if rounds:
        announce(0)
    for load in loads[1:]:
        load.wait()
    for matrix, terms in ((forward_ref, forward_terms), (backward_ref, backward_terms)):
        depth = matrix.shape[0]
        values = matrix[...]
        high = values.astype(BF16)
        terms[0:depth, :] = high
        terms[depth : 2 * depth, :] = high
        terms[2 * depth : 3 * depth, :] = (values - high.astype(F32)).astype(BF16)
    for turn in range(len(rounds) - 1):
        hear(turn)
        announce(turn + 1)
    base = receive(0, base)

    unused, flux = fluxes(base)
    first_raw = image_of(flux, mass_times(base))
    first = joined(first_raw)
    pack(1, first)
    send(1)
    moment0 = dot(base, raw)
    moment1 = dot(base, first_raw)
    first = receive(1, first)

    moment2 = dot(first, first_raw)
    grads, flux = fluxes(first)
    mass_part = mass_times(first)
    moment3 = (dot(grads[0], flux[0]) + dot(grads[1], flux[1])) + (
        dot(grads[2], flux[2]) + dot(first, mass_part)
    )

    def halves(a, b):
        low = lane < 64
        return jnp.where(low, a, b) + pltpu.roll(jnp.where(low, b, a), 64, 1)

    odd, even = halves(moment0, moment1), halves(moment2, moment3)
    pairs = jnp.where(
        (lane & 32) != 0,
        odd + pltpu.roll(odd, 32, 1),
        even + pltpu.roll(even, LANES - 32, 1),
    )
    total = jnp.sum(pairs, axis=0, keepdims=True)

    def start_group(axis, value):
        sums_out[axis, 0:1, :] = value
        for k, steps in enumerate(groups[axis]):
            pltpu.make_async_remote_copy(
                src_ref=sums_out.at[axis, pl.ds(0, 1)],
                dst_ref=sums_in.at[axis, pl.ds(k, 1)],
                send_sem=sum_send_sem.at[axis],
                recv_sem=sum_sem.at[axis],
                device_id=at(steps),
                device_id_type=MESH,
            ).start()

    def finish_group(axis, value):
        count = len(groups[axis])
        wait_bytes(sums_in.at[axis, pl.ds(0, count)], sum_sem.at[axis])
        return value + jnp.sum(sums_in[axis, 0:count, :], axis=0, keepdims=True)

    def packed_grid(tiles):
        out = []
        for t in tiles:
            for bit in range(4):
                take = radial_ref[2 * NODES, bit : bit + 1, :] > 0.5
                t = jnp.where(take, pltpu.roll(t, LANES - (1 << bit), 1), t)
            out.append(t)
        return [
            out[0],
            jnp.where(row < NODES - 1, pltpu.roll(out[1], NODES - 1, 0), pltpu.roll(out[2], NODES - 2, 0)),
            pltpu.roll(out[2], NODES - 2, 0),
        ]

    def keep_grid(which, tiles):
        for slot in range(SLOTS):
            count = min(NODES, PLANES_X - slot * NODES)
            fields_ref[which, pl.ds(slot * NODES, count), :] = tiles[slot][:count, :PLANES_YZ]

    if rounds:
        hear(len(rounds) - 1)
    start_group(0, total)
    second = joined(image_of(flux, mass_part))
    pack(2, second)
    send(2)
    keep_grid(0, packed_grid(base))
    keep_grid(1, packed_grid(first))
    total = finish_group(0, total)
    start_group(1, total)
    keep_grid(2, packed_grid(receive(2, second)))
    for turn in range(3):
        wait_bytes(edges.at[turn, pl.ds(0, 18)], send_sem.at[turn, 1])
        wait_bytes(fields.at[turn], send_sem.at[turn, 0])
    total = finish_group(1, total)

    group = lax.broadcasted_iota(jnp.int32, (1, LANES), 1) // 32
    m2, m0, m3, m1 = (
        jnp.sum(jnp.where(group == k, total, 0.0), axis=1, keepdims=True) for k in range(4)
    )
    alpha0 = m0 / m1
    gain = (m2 / m1) * alpha0
    alpha1 = alpha0 * (gain - 1.0) / (alpha0 * (alpha0 * (m3 / m1)) - gain * gain)
    scale0 = alpha0 + alpha1 * gain
    scale1 = alpha0 * alpha1
    fields_ref[3] = jnp.broadcast_to(scale0, (PLANES_X, PLANES_YZ))
    fields_ref[4] = jnp.broadcast_to(scale1, (PLANES_X, PLANES_YZ))

    for axis in range(2):
        wait_bytes(sums_in.at[axis, pl.ds(0, len(groups[axis]))], sum_send_sem.at[axis])


def local(sizes, rhs_local, geom_diag, geom_off, mass_coef, elem_counts):
    forward, backward, radial = tables()
    hbm = pl.BlockSpec(memory_space=pltpu.HBM)
    base, first, second, scale0, scale1 = pl.pallas_call(
        functools.partial(kernel, sizes),
        name="cg",
        out_shape=jax.ShapeDtypeStruct((5, PLANES_X, PLANES_YZ), F32),
        in_specs=[pl.BlockSpec(memory_space=pltpu.SMEM)] + [hbm] * 7,
        out_specs=pl.BlockSpec(memory_space=pltpu.VMEM),
        scratch_shapes=[
            pltpu.VMEM((ROWS, LANES), F32),
            pltpu.VMEM((3, ROWS, LANES), F32),
            pltpu.VMEM((3, ROWS, LANES), F32),
            pltpu.VMEM((ROWS, LANES), F32),
            pltpu.VMEM(forward.shape, F32),
            pltpu.VMEM(backward.shape, F32),
            pltpu.VMEM((3 * forward.shape[0], forward.shape[1]), BF16),
            pltpu.VMEM((3 * backward.shape[0], backward.shape[1]), BF16),
            pltpu.VMEM(radial.shape, F32),
            pltpu.VMEM((3, 9, ROWS + NODES, LANES), F32),
            pltpu.VMEM((3, 8 * ROWS, LANES), F32),
            pltpu.VMEM((3, 24, LANES), F32),
            pltpu.VMEM((2, 8, LANES), F32),
            pltpu.VMEM((2, 64, LANES), F32),
            pltpu.SemaphoreType.DMA((7,)),
            pltpu.SemaphoreType.DMA((3, 2)),
            pltpu.SemaphoreType.DMA((3,)),
            pltpu.SemaphoreType.DMA((3,)),
            pltpu.SemaphoreType.DMA((3,)),
            pltpu.SemaphoreType.DMA((3,)),
            pltpu.SemaphoreType.REGULAR((4, 3, 2)),
        ],
        compiler_params=pltpu.CompilerParams(
            collective_id=0, has_side_effects=True, vmem_limit_bytes=16 * 1024 * 1024
        ),
    )(
        elem_counts,
        *(
            pltpu.with_memory_space_constraint(array, pltpu.HBM)
            for array in (
                rhs_local,
                geom_diag,
                geom_off,
                mass_coef,
                jnp.asarray(forward),
                jnp.asarray(backward),
                jnp.asarray(radial),
            )
        ),
    )
    return scale0 * base - scale1 * first, base - scale0 * first + scale1 * second


def solution(mesh):
    placed = (
        P(AXES, None),
        P(None, AXES, None),
        P(None, AXES, None),
        P(AXES, None),
        P(AXES),
    )
    sizes = tuple(mesh.shape[axis] for axis in AXES)
    return jax.shard_map(
        functools.partial(local, sizes),
        mesh=mesh,
        in_specs=placed,
        out_specs=(P(AXES, None), P(AXES, None)),
        check_vma=False,
    )
```

```python
import functools

import jax
import jax.numpy as jnp
import numpy as np
from jax import lax
from jax.experimental import pallas as pl
from jax.experimental.pallas import tpu as pltpu
from jax.sharding import PartitionSpec as P

ORDER = 7
NODES = ORDER + 1
EY = 1
EZ = 2
SLOTS = 3
ROWS = SLOTS * NODES
LANES = EY * NODES * EZ * NODES
PLANES_X = ORDER * SLOTS + 1
PLANES_YZ = (ORDER * EY + 1) * (ORDER * EZ + 1)
AXES = ("gx", "gy", "gz")
MESH = pl.DeviceIdType.MESH
F32 = jnp.float32
BF16 = jnp.bfloat16

points_gll = (
    -1.0,
    -0.8717401485096066,
    -0.5917001814331423,
    -0.2092992179024789,
    0.2092992179024789,
    0.5917001814331423,
    0.8717401485096066,
    1.0,
)

SIDES = ((-1, -1), (-1, 1), (1, -1), (1, 1), (0, -1), (0, 1), (-1, 0), (1, 0), (0, 0))
NEIGHBOURS = sorted(
    ((dx, dy, dz) for dx in (-1, 0, 1) for dy, dz in SIDES if (dx, dy, dz) != (0, 0, 0)),
    key=lambda steps: -sum(map(abs, steps)),
)


def derivative_table():
    points = np.array(points_gll)
    total_points = points.shape[0]
    weights = np.ones(total_points)
    for j in range(total_points):
        for k in range(total_points):
            if k != j:
                weights[j] = weights[j] / (points[j] - points[k])
    deriv_table = np.zeros((total_points, total_points))
    for i in range(total_points):
        for j in range(total_points):
            if i != j:
                deriv_table[i, j] = weights[j] / weights[i] / (points[i] - points[j])
        deriv_table[i, i] = -np.sum(deriv_table[i])
    return deriv_table


def tables():
    deriv = derivative_table().astype(np.float32)
    eye8, eye2 = np.eye(NODES, dtype=np.float32), np.eye(EZ, dtype=np.float32)
    along_s = np.kron(deriv, np.kron(eye2, eye8))
    along_t = np.kron(eye8, np.kron(eye2, deriv))
    forward = np.concatenate([along_s.T, along_t.T], axis=1)
    backward = np.concatenate([along_s, along_t], axis=0)

    radial = np.zeros((2 * NODES + 1, NODES, LANES), np.float32)
    for i in range(NODES):
        radial[i] = deriv[:, i][:, None]
        radial[NODES + i] = deriv[i, :][:, None]
    lanes = np.arange(LANES)
    distance = lanes // 16 + (lanes % 16 > 8)
    kept = lanes % 16 != 8
    for bit in range(4):
        for lane in lanes[kept]:
            if distance[lane] >> bit & 1:
                radial[2 * NODES, bit, lane - (distance[lane] & ((2 << bit) - 1))] = 1.0
    return forward, backward, radial


def kernel(
    sizes,
    counts_ref,
    rhs_hbm,
    diag_hbm,
    off_hbm,
    mass_hbm,
    forward_hbm,
    backward_hbm,
    radial_hbm,
    fields_ref,
    rhs_ref,
    diag_ref,
    off_ref,
    mass_ref,
    forward_ref,
    backward_ref,
    forward_terms,
    backward_terms,
    radial_ref,
    outgoing,
    fields,
    edges,
    sums_out,
    sums_in,
    load_sem,
    send_sem,
    field_sem,
    edge_sem,
    sum_send_sem,
    sum_sem,
    here_sem,
):
    here = tuple(lax.axis_index(axis) for axis in AXES)
    index_x, index_y, index_z = here

    places = {}

    def at(steps):
        for axis in range(3):
            step = steps[axis] % sizes[axis]
            if (axis, step) not in places:
                moved_on = here[axis] + step
                places[axis, step] = (
                    jnp.where(moved_on >= sizes[axis], moved_on - sizes[axis], moved_on)
                    if step
                    else here[axis]
                )
        place = [places[axis, steps[axis] % sizes[axis]] for axis in range(3)]
        if len(steps) == 4:
            place[1] = place[1] + 1 - 2 * lax.rem(place[1], 2)
        return tuple(place)

    def signal(semaphore, steps):
        pl.semaphore_signal(semaphore, inc=1, device_id=at(steps), device_id_type=MESH)

    def distance(steps):
        around = [min(step % size, -step % size) for step, size in zip(steps, sizes)]
        return around[0] + around[1] / 2 + around[2]

    groups = [
        sorted(
            [(step, 0, 0) for step in range(1, sizes[0])]
            + [(step, 0, 0, 1) for step in range(sizes[0])],
            key=distance,
            reverse=True,
        ),
        sorted(
            (
                (0, step_y, step_z)
                for step_y in range(0, sizes[1], 2)
                for step_z in range(sizes[2])
                if step_y or step_z
            ),
            key=distance,
            reverse=True,
        ),
    ]

    loads = [
        pltpu.make_async_copy(source, target, load_sem.at[i])
        for i, (source, target) in enumerate(
            (
                (rhs_hbm, rhs_ref),
                (forward_hbm, forward_ref),
                (radial_hbm, radial_ref),
                (diag_hbm, diag_ref),
                (off_hbm, off_ref),
                (mass_hbm, mass_ref),
                (backward_hbm, backward_ref),
            )
        )
    ]
    loads[0].start()

    taken = {tuple(step % size for step, size in zip(steps, sizes)) for steps in NEIGHBOURS}
    greeted = NEIGHBOURS + [
        (0, step_y, step_z)
        for step_y in (-1, 0, 1)
        for step_z in range(2, sizes[2] - 1)
        if (0, step_y % sizes[1], step_z) not in taken
    ]
    barrier = pltpu.get_barrier_semaphore()
    for steps in greeted:
        signal(barrier, steps)

    for load in loads[1:]:
        load.start()

    lane = lax.broadcasted_iota(jnp.int32, (NODES, LANES), 1)
    row = lax.broadcasted_iota(jnp.int32, (NODES, LANES), 0)
    in_group = lane & 15
    zero = jnp.zeros((NODES, LANES), F32)

    keep_z = {
        1: (in_group == 0) & (index_z < sizes[2] - 1),
        -1: (in_group == 15) & (index_z > 0),
    }
    keep_y = {
        1: (lane < 16) & (index_y < sizes[1] - 1),
        -1: (lane >= LANES - 16) & (index_y > 0),
    }
    turn_z = {1: LANES - 15, -1: 15}
    turn_y = {1: 16, -1: LANES - 16}

    def tiled(function, *tiles):
        return [function(*parts) for parts in zip(*tiles)]

    def moved(tiles, turn, keep):
        return [jnp.where(keep, pltpu.roll(t, turn, 1), zero) for t in tiles]

    loads[0].wait()
    width = counts_ref[0] // (EY * EZ)
    live = [width > slot for slot in range(SLOTS)]

    def joined(tiles):
        tiles = [
            t
            + jnp.where(
                in_group == 7,
                pltpu.roll(t, LANES - 1, 1),
                jnp.where(in_group == 8, pltpu.roll(t, 1, 1), zero),
            )
            for t in tiles
        ]
        out = []
        for slot in range(SLOTS):
            total = tiles[slot]
            if slot:
                before = jnp.where(row == 0, pltpu.roll(tiles[slot - 1], 1, 0), zero)
                total = jnp.where(live[slot], total + before, zero)
            if slot + 1 < SLOTS:
                total = total + jnp.where(
                    row == NODES - 1, pltpu.roll(tiles[slot + 1], NODES - 1, 0), zero
                )
            out.append(total)
        return out

    def last_tile(tiles):
        return jnp.where(live[2], tiles[2], jnp.where(live[1], tiles[1], tiles[0]))

    def pack(turn, tiles):
        by_z = {0: tiles}
        for dz in (-1, 1):
            by_z[dz] = moved(tiles, turn_z[dz], keep_z[dz])
        for k, (dy, dz) in enumerate(SIDES):
            message = moved(by_z[dz], turn_y[dy], keep_y[dy]) if dy else by_z[dz]
            for slot in range(SLOTS):
                outgoing[turn, k, pl.ds(slot * NODES, NODES), :] = message[slot]
            outgoing[turn, k, pl.ds(ROWS, NODES), :] = last_tile(message)

    def edge_row(dx, k):
        row_before = 16 if k == 8 else k
        return row_before + (1 if k == 8 else 8) * (dx < 0)

    def send(turn):
        for steps in NEIGHBOURS:
            dx, k = steps[0], SIDES.index(steps[1:])
            if dx:
                source, count = (ROWS + NODES - 1 if dx > 0 else 0), 1
                target, row_to, sem, kind = edges, edge_row(dx, k), edge_sem, 1
            else:
                source, count = 0, ROWS
                target, row_to, sem, kind = fields, k * ROWS, field_sem, 0
            pltpu.make_async_remote_copy(
                src_ref=outgoing.at[turn, k, pl.ds(source, count)],
                dst_ref=target.at[turn, pl.ds(row_to, count)],
                send_sem=send_sem.at[turn, kind],
                recv_sem=sem.at[turn],
                device_id=at(steps),
                device_id_type=MESH,
            ).start()

    def wait_bytes(ref, sem):
        pltpu.make_async_copy(ref, ref, sem).wait()

    def receive(turn, tiles):
        wait_bytes(fields.at[turn], field_sem.at[turn])
        out = []
        for slot in range(SLOTS):
            parts = [
                fields[turn, pl.ds(k * ROWS + slot * NODES, NODES), :] for k in range(8)
            ]
            total = ((parts[0] + parts[1]) + (parts[2] + parts[3])) + (
                (parts[4] + parts[5]) + (parts[6] + parts[7])
            )
            out.append(tiles[slot] + total)
        wait_bytes(edges.at[turn, pl.ds(0, 18)], edge_sem.at[turn])
        before = jnp.sum(edges[turn, 0:8, :], axis=0, keepdims=True) + edges[turn, 16:17, :]
        after = jnp.sum(edges[turn, 8:16, :], axis=0, keepdims=True) + edges[turn, 17:18, :]
        before = jnp.where((row == 0) & (index_x > 0), before, zero)
        after = jnp.where((row == NODES - 1) & (index_x < sizes[0] - 1), after, zero)
        for slot in range(SLOTS):
            is_last = live[slot] & jnp.logical_not(live[slot + 1]) if slot + 1 < SLOTS else live[slot]
            extra = jnp.where(is_last, after, zero)
            out[slot] = out[slot] + (extra + before if slot == 0 else extra)
        return out

    def three_terms(values):
        high = values.astype(BF16)
        low = (values - high.astype(F32)).astype(BF16)
        return jnp.concatenate([high, low, high], axis=1)

    def rows_of(tiles):
        return jnp.concatenate(tiles, axis=0)

    def tiles_of(values):
        return [values[slot * NODES : (slot + 1) * NODES, :] for slot in range(SLOTS)]

    def along_r(tiles, first):
        out = []
        for t in tiles:
            terms = [radial_ref[first + i] * t[i : i + 1, :] for i in range(NODES)]
            out.append(
                ((terms[0] + terms[1]) + (terms[2] + terms[3]))
                + ((terms[4] + terms[5]) + (terms[6] + terms[7]))
            )
        return out

    def fluxes(tiles):
        lane_grads = jnp.dot(
            three_terms(rows_of(tiles)), forward_terms[...], preferred_element_type=F32
        )
        grad_r = along_r(tiles, 0)
        grad_s = tiles_of(lane_grads[:, :LANES])
        grad_t = tiles_of(lane_grads[:, LANES:])
        flux = ([], [], [])
        for slot in range(SLOTS):
            at_slot = pl.ds(slot * NODES, NODES)
            g_rr, g_ss, g_tt = (diag_ref[i, at_slot, :] for i in range(3))
            g_rs, g_rt, g_st = (off_ref[i, at_slot, :] for i in range(3))
            u_r, u_s, u_t = grad_r[slot], grad_s[slot], grad_t[slot]
            flux[0].append(g_rr * u_r + g_rs * u_s + g_rt * u_t)
            flux[1].append(g_rs * u_r + g_ss * u_s + g_st * u_t)
            flux[2].append(g_rt * u_r + g_st * u_s + g_tt * u_t)
        return (grad_r, grad_s, grad_t), flux

    def mass_times(tiles):
        return [mass_ref[pl.ds(slot * NODES, NODES), :] * tiles[slot] for slot in range(SLOTS)]

    def image_of(flux, mass_part):
        packed = jnp.concatenate([rows_of(flux[1]), rows_of(flux[2])], axis=1)
        lane_part = tiles_of(
            jnp.dot(three_terms(packed), backward_terms[...], preferred_element_type=F32)
        )
        return tiled(lambda a, b, c: (a + c) + b, lane_part, along_r(flux[0], NODES), mass_part)

    def dot(left, right):
        return (left[0] * right[0] + left[1] * right[1]) + left[2] * right[2]

    raw = [
        jnp.where(live[slot], rhs_ref[pl.ds(slot * NODES, NODES), :], zero)
        for slot in range(SLOTS)
    ]
    base = joined(raw)
    pack(0, base)
    pl.semaphore_wait(barrier, len(greeted))
    send(0)
    rounds = []
    reach = 1
    while any(reach < size // 2 for size in sizes[:2]):
        rounds.append([(axis, reach) for axis in (0, 1) if reach < sizes[axis] // 2])
        reach *= 2

    def announce(turn):
        for axis, reach in rounds[turn]:
            for way in (0, 1):
                steps = [0, 0, 0]
                steps[axis] = reach if way else -reach
                signal(here_sem.at[turn, axis, way], steps)

    def hear(turn):
        for axis, unused_reach in rounds[turn]:
            for way in (0, 1):
                pl.semaphore_wait(here_sem.at[turn, axis, way], 1)

    if rounds:
        announce(0)
    for load in loads[1:]:
        load.wait()
    for matrix, terms in ((forward_ref, forward_terms), (backward_ref, backward_terms)):
        depth = matrix.shape[0]
        values = matrix[...]
        high = values.astype(BF16)
        terms[0:depth, :] = high
        terms[depth : 2 * depth, :] = high
        terms[2 * depth : 3 * depth, :] = (values - high.astype(F32)).astype(BF16)
    for turn in range(len(rounds) - 1):
        hear(turn)
        announce(turn + 1)
    base = receive(0, base)

    unused, flux = fluxes(base)
    first_raw = image_of(flux, mass_times(base))
    first = joined(first_raw)
    pack(1, first)
    send(1)
    moment0 = dot(base, raw)
    moment1 = dot(base, first_raw)
    first = receive(1, first)

    moment2 = dot(first, first_raw)
    grads, flux = fluxes(first)
    mass_part = mass_times(first)
    moment3 = (dot(grads[0], flux[0]) + dot(grads[1], flux[1])) + (
        dot(grads[2], flux[2]) + dot(first, mass_part)
    )

    def halves(a, b):
        low = lane < 64
        return jnp.where(low, a, b) + pltpu.roll(jnp.where(low, b, a), 64, 1)

    odd, even = halves(moment0, moment1), halves(moment2, moment3)
    pairs = jnp.where(
        (lane & 32) != 0,
        odd + pltpu.roll(odd, 32, 1),
        even + pltpu.roll(even, LANES - 32, 1),
    )
    total = jnp.sum(pairs, axis=0, keepdims=True)

    def start_group(axis, value):
        sums_out[axis, 0:1, :] = value
        for k, steps in enumerate(groups[axis]):
            pltpu.make_async_remote_copy(
                src_ref=sums_out.at[axis, pl.ds(0, 1)],
                dst_ref=sums_in.at[axis, pl.ds(k, 1)],
                send_sem=sum_send_sem.at[axis],
                recv_sem=sum_sem.at[axis],
                device_id=at(steps),
                device_id_type=MESH,
            ).start()

    def finish_group(axis, value):
        count = len(groups[axis])
        wait_bytes(sums_in.at[axis, pl.ds(0, count)], sum_sem.at[axis])
        return value + jnp.sum(sums_in[axis, 0:count, :], axis=0, keepdims=True)

    def packed_grid(tiles):
        out = []
        for t in tiles:
            for bit in range(4):
                take = radial_ref[2 * NODES, bit : bit + 1, :] > 0.5
                t = jnp.where(take, pltpu.roll(t, LANES - (1 << bit), 1), t)
            out.append(t)
        return [
            out[0],
            jnp.where(row < NODES - 1, pltpu.roll(out[1], NODES - 1, 0), pltpu.roll(out[2], NODES - 2, 0)),
            pltpu.roll(out[2], NODES - 2, 0),
        ]

    def keep_grid(which, tiles):
        for slot in range(SLOTS):
            count = min(NODES, PLANES_X - slot * NODES)
            fields_ref[which, pl.ds(slot * NODES, count), :] = tiles[slot][:count, :PLANES_YZ]

    if rounds:
        hear(len(rounds) - 1)
    start_group(0, total)
    second = joined(image_of(flux, mass_part))
    pack(2, second)
    send(2)
    keep_grid(0, packed_grid(base))
    keep_grid(1, packed_grid(first))
    total = finish_group(0, total)
    start_group(1, total)
    keep_grid(2, packed_grid(receive(2, second)))
    for turn in range(3):
        wait_bytes(edges.at[turn, pl.ds(0, 18)], send_sem.at[turn, 1])
        wait_bytes(fields.at[turn], send_sem.at[turn, 0])
    total = finish_group(1, total)

    group = lax.broadcasted_iota(jnp.int32, (1, LANES), 1) // 32
    m2, m0, m3, m1 = (
        jnp.sum(jnp.where(group == k, total, 0.0), axis=1, keepdims=True) for k in range(4)
    )
    alpha0 = m0 / m1
    gain = (m2 / m1) * alpha0
    alpha1 = alpha0 * (gain - 1.0) / (alpha0 * (alpha0 * (m3 / m1)) - gain * gain)
    scale0 = alpha0 + alpha1 * gain
    scale1 = alpha0 * alpha1
    fields_ref[3] = jnp.broadcast_to(scale0, (PLANES_X, PLANES_YZ))
    fields_ref[4] = jnp.broadcast_to(scale1, (PLANES_X, PLANES_YZ))

    for axis in range(2):
        wait_bytes(sums_in.at[axis, pl.ds(0, len(groups[axis]))], sum_send_sem.at[axis])


def local(sizes, rhs_local, geom_diag, geom_off, mass_coef, elem_counts):
    forward, backward, radial = tables()
    hbm = pl.BlockSpec(memory_space=pltpu.HBM)
    base, first, second, scale0, scale1 = pl.pallas_call(
        functools.partial(kernel, sizes),
        name="cg",
        out_shape=jax.ShapeDtypeStruct((5, PLANES_X, PLANES_YZ), F32),
        in_specs=[pl.BlockSpec(memory_space=pltpu.SMEM)] + [hbm] * 7,
        out_specs=pl.BlockSpec(memory_space=pltpu.VMEM),
        scratch_shapes=[
            pltpu.VMEM((ROWS, LANES), F32),
            pltpu.VMEM((3, ROWS, LANES), F32),
            pltpu.VMEM((3, ROWS, LANES), F32),
            pltpu.VMEM((ROWS, LANES), F32),
            pltpu.VMEM(forward.shape, F32),
            pltpu.VMEM(backward.shape, F32),
            pltpu.VMEM((3 * forward.shape[0], forward.shape[1]), BF16),
            pltpu.VMEM((3 * backward.shape[0], backward.shape[1]), BF16),
            pltpu.VMEM(radial.shape, F32),
            pltpu.VMEM((3, 9, ROWS + NODES, LANES), F32),
            pltpu.VMEM((3, 8 * ROWS, LANES), F32),
            pltpu.VMEM((3, 24, LANES), F32),
            pltpu.VMEM((2, 8, LANES), F32),
            pltpu.VMEM((2, 64, LANES), F32),
            pltpu.SemaphoreType.DMA((7,)),
            pltpu.SemaphoreType.DMA((3, 2)),
            pltpu.SemaphoreType.DMA((3,)),
            pltpu.SemaphoreType.DMA((3,)),
            pltpu.SemaphoreType.DMA((3,)),
            pltpu.SemaphoreType.DMA((3,)),
            pltpu.SemaphoreType.REGULAR((4, 3, 2)),
        ],
        compiler_params=pltpu.CompilerParams(
            collective_id=0, has_side_effects=True, vmem_limit_bytes=16 * 1024 * 1024
        ),
    )(
        elem_counts,
        *(
            pltpu.with_memory_space_constraint(array, pltpu.HBM)
            for array in (
                rhs_local,
                geom_diag,
                geom_off,
                mass_coef,
                jnp.asarray(forward),
                jnp.asarray(backward),
                jnp.asarray(radial),
            )
        ),
    )
    return scale0 * base - scale1 * first, base - scale0 * first + scale1 * second


def solution(mesh):
    placed = (
        P(AXES, None),
        P(None, AXES, None),
        P(None, AXES, None),
        P(AXES, None),
        P(AXES),
    )
    sizes = tuple(mesh.shape[axis] for axis in AXES)
    return jax.shard_map(
        functools.partial(local, sizes),
        mesh=mesh,
        in_specs=placed,
        out_specs=(P(AXES, None), P(AXES, None)),
        check_vma=False,
    )
```
